32 devices in a mesh: coef: 1, pair: 32 (over z, y, x, core).
Axes of the slice: x: 2, y: 2, z: 4, core: 2. Of those that a mesh axis runs over, the one named last changes fastest.
Arguments:
- integrals: bfloat16 [128, 32, 8192], P(('coef', 'pair')), may hold values from -66 to 66
- coefficients: bfloat16 [2, 8192, 384], P(None, ('coef', 'pair')), may hold values from -0.0625 to 0.0625
- shell_starts: int32 [8], replicated, may hold values from 0 to 8188, as said below
- pair_ids: int32 [1, 128], P('coef'), may hold values from 0 to 127, each once within a row
Outputs:
- half_ints: bfloat16 [2, 384, 384, 128], P(None, 'pair', None, 'coef')
The draws below stay inside these ranges and needn't reach their ends.
Inputs may be any that keep to these rules, and one draw needn't show every extreme that they name: `shell_starts`: distinct multiples of 4.
All inputs are finite; a program needn't handle non-finite values.
Results may differ from the reference program's by a relative error of at most 0.0049.
Values may be sent and summed in bfloat16 or wider, within the bound.
No kernel may reach another device: no remote copies, remote signals or barrier semaphores. Data moves between devices by JAX's collectives and lax.ppermute only.
A program may use at most 64 MiB of HBM per device.

```python
import jax
import jax.numpy as jnp
from jax import lax

NAO = 8192
NOCC = 384
SHW = 4
BS = 8
MB = 32
KP_COEF = 128
KPAIRS = 128
N_COEF = 1


def draw_shell_starts(key, part):
    total_shells = NAO // SHW
    middle = jax.random.permutation(jax.random.fold_in(key, 11), total_shells - 2)[:BS - 2] + 1
    ends = jnp.array([0, total_shells - 1], dtype=jnp.int32)
    chosen = jnp.concatenate([ends, middle.astype(jnp.int32)])
    order = jax.random.permutation(jax.random.fold_in(key, 12), BS)
    return (chosen[order] * SHW).astype(jnp.int32)


def levels(stream_key, dims, split, low, top_value):
    loudness, own = 1.0, jax.random.fold_in(stream_key, 6)
    for dim, parts in split:
        draws = jnp.exp(jax.random.uniform(jax.random.fold_in(own, dim), (parts,), jnp.float32, low / len(split), top_value / len(split)))
        loudness = loudness * jnp.repeat(draws, dims[dim] // parts).reshape([-1 if axis == dim else 1 for axis in range(len(dims))])
    return loudness


def noise(own_key, extent, width, most, split=(), kind=jnp.bfloat16):
    values = width * jax.random.normal(own_key, extent, jnp.float32)
    if split:
        values = values * levels(own_key, extent, split, -0.22, 0.18)
    return jnp.clip(values, -most, most).astype(kind)


def setup_inputs(seed: int = 0) -> dict:
    streams_of = jax.random.split(jax.random.key(seed), 5)
    integrals = noise(streams_of[0], (KPAIRS, MB, NAO), 11.0, 66.0, ((0, 32),))
    coefficients = noise(streams_of[1], (2, NAO, NOCC), NAO ** -0.5, 0.0625, ((1, 32),))
    shell_starts = draw_shell_starts(jax.random.fold_in(streams_of[4], 71), 0)
    pair_ids = jax.vmap(lambda own: jax.random.permutation(own, KP_COEF))(jax.random.split(streams_of[3], N_COEF)).reshape((N_COEF, KP_COEF)).astype(jnp.int32)
    return dict(integrals=integrals, coefficients=coefficients, shell_starts=shell_starts, pair_ids=pair_ids)


def reference(integrals, coefficients, shell_starts, pair_ids):
    offsets = jnp.arange(SHW, dtype=jnp.int32)
    batch_index = (shell_starts[:, None] + offsets[None, :]).reshape(-1).astype(jnp.int32)
    batch_coef = jnp.take(coefficients, batch_index, axis=1)
    coef_real = batch_coef[0].astype(jnp.float32)
    coef_imag = batch_coef[1].astype(jnp.float32)
    blocks = integrals.reshape(N_COEF, KP_COEF * MB, NAO)

    def transform(pair_item):
        int_block, pair_order = pair_item
        half_real = jnp.dot(int_block, coefficients[0], preferred_element_type=jnp.float32).astype(jnp.bfloat16)
        half_imag = jnp.dot(int_block, coefficients[1], preferred_element_type=jnp.float32).astype(jnp.bfloat16)
        half_real = half_real.reshape(KP_COEF, MB, NOCC).astype(jnp.float32)
        half_imag = half_imag.reshape(KP_COEF, MB, NOCC).astype(jnp.float32)
        real_part = jnp.einsum("mi,kmj->kij", coef_real, half_real) + jnp.einsum("mi,kmj->kij", coef_imag, half_imag)
        imag_part = jnp.einsum("mi,kmj->kij", coef_real, half_imag) - jnp.einsum("mi,kmj->kij", coef_imag, half_real)
        stacked = jnp.stack([real_part, imag_part]).astype(jnp.bfloat16)
        placed = jnp.zeros((2, KP_COEF, NOCC, NOCC), jnp.bfloat16).at[:, pair_order].set(stacked)
        return placed

    result = lax.map(transform, (blocks, pair_ids))
    return jnp.transpose(result, (1, 3, 4, 0, 2)).reshape(2, NOCC, NOCC, N_COEF * KP_COEF)
```

```python
import functools

import jax
import jax.numpy as jnp
from jax import lax
from jax.experimental import pallas as pl
from jax.experimental.pallas import tpu as pltpu
from jax.sharding import PartitionSpec as P

SHW = 4
LANES = 128
F32, BF16 = jnp.float32, jnp.bfloat16
VMEM_LIMIT = 40 * 1024 * 1024


class Grid:
    def __init__(self, n_pair):
        assert n_pair % 8 == 0
        self.nz = n_pair // 8
        self.ring = 2 * self.nz

    def device(self, q, y, c):
        turned = q >= self.nz
        z = jnp.where(turned, self.ring - 1 - q, q)
        x = turned.astype(jnp.int32)
        return ((z * 2 + y) * 2 + x) * 2 + c

    def number(self, q, y, c):
        z, x = (q, 0) if q < self.nz else (self.ring - 1 - q, 1)
        return ((z * 2 + y) * 2 + x) * 2 + c

    def moves(self, target):
        return [
            (self.number(q, y, c), self.number(*target(q, y, c)))
            for q in range(self.ring)
            for y in range(2)
            for c in range(2)
        ]

    def around(self, way):
        return self.moves(lambda q, y, c: ((q + (way if c == 0 else -way)) % self.ring, y, c))

    def across_y(self):
        return self.moves(lambda q, y, c: (q, 1 - y, c))

    def across_core(self):
        return self.moves(lambda q, y, c: (q, y, 1 - c))

    def offsets(self):
        found = [0]
        for step in range(1, self.nz):
            found += [-step, step]
        return found + [-self.nz]


def gather_chips(grid, first, later):
    send = functools.partial(lax.ppermute, axis_name="pair")
    around = {-1: grid.around(1), 1: grid.around(-1)}
    over_y = grid.across_y()
    pairs = {0: jnp.concatenate([first, send(first, perm=over_y)], axis=0)}
    singles = {0: later}
    for step in range(1, grid.nz + 1):
        for side in (-1, 1):
            if side == 1 and step == grid.nz:
                continue
            offset = side * step
            singles[offset] = send(singles[offset - side], perm=around[side])
            pairs[offset] = send(pairs[offset - side], perm=around[side])
    mirrored = {offset: send(block, perm=over_y) for offset, block in singles.items()}
    return pairs, singles, mirrored


def vmem(count):
    return [pl.BlockSpec(memory_space=pltpu.VMEM)] * count


PARAMS = pltpu.CompilerParams(vmem_limit_bytes=VMEM_LIMIT)


def first_product(source, own_ints, other_ints, batch_column, total, parts, last):
    width = parts[0][0].shape[1]
    rows = own_ints.shape[0]
    batch_rows = batch_column.shape[0]
    depth = min(block.shape[0] // len(slots) for block, slots in parts)
    begins = total is None

    def body(source_ref, own_ref, other_ref, batch_ref, *refs):
        refs = list(refs)
        total_ref = None if begins else refs.pop(0)
        block_refs, out_refs = refs[: len(parts)], refs[len(parts):]
        running = None if begins else total_ref[...]
        for ref, (_, slots) in zip(block_refs, parts):
            for place, slot in enumerate(slots):
                start = pl.multiple_of(source_ref[slot] * depth, depth)
                columns = pl.ds(start, depth)
                position = lax.broadcasted_iota(jnp.int32, (batch_rows, depth), 1) + start
                picks = (batch_ref[...] == position).astype(F32).astype(BF16)
                left = jnp.concatenate([own_ref[:, columns], other_ref[:, columns], picks], axis=0)
                term = jnp.dot(left, ref[place * depth:(place + 1) * depth, :], preferred_element_type=F32)
                running = term if running is None else running + term
        if last:
            out_refs[0][...] = running[:rows].astype(BF16)
            out_refs[1][...] = running[rows:].astype(BF16)
        else:
            out_refs[0][...] = running

    high = 2 * rows + batch_rows
    if last:
        shapes = [jax.ShapeDtypeStruct((rows, width), BF16), jax.ShapeDtypeStruct((high - rows, width), BF16)]
    else:
        shapes = [jax.ShapeDtypeStruct((high, width), F32)]
    operands = ([] if begins else [total]) + [block for block, _ in parts]
    return pl.pallas_call(
        body,
        out_shape=shapes,
        in_specs=[pl.BlockSpec(memory_space=pltpu.SMEM)] + vmem(3 + len(operands)),
        out_specs=vmem(len(shapes)),
        compiler_params=PARAMS,
        name="first_product",
    )(source, own_ints, other_ints, batch_column, *operands)


def weights(where, own_batch, other_batch, slots, share):
    batch_rows, width = own_batch.shape
    high = 2 * slots * 2 * share

    def body(where_ref, own_ref, other_ref, own_out, other_out):
        me = where_ref[0]
        core = lax.rem(me, 2)
        row = lax.broadcasted_iota(jnp.int32, (high, width), 0)
        column = lax.broadcasted_iota(jnp.int32, (high, width), 1)
        half = lax.div(row, high // 2)
        wanted = (me - core + lax.rem(core + half, 2)) * share + lax.rem(row, share)
        chosen = (column == wanted).astype(F32).astype(BF16)
        deep = slots * batch_rows
        repeat = (
            lax.broadcasted_iota(jnp.int32, (batch_rows, deep), 0)
            == lax.rem(lax.broadcasted_iota(jnp.int32, (batch_rows, deep), 1), batch_rows)
        ).astype(F32).astype(BF16)

        def spread(ref):
            picked = lax.dot_general(chosen, ref[...], (((1,), (1,)), ((), ())), preferred_element_type=F32)
            return jnp.dot(picked.astype(BF16), repeat, preferred_element_type=F32)

        row = lax.broadcasted_iota(jnp.int32, (high, deep), 0)
        column = lax.broadcasted_iota(jnp.int32, (high, deep), 1)
        keep = lax.rem(lax.div(row, 2 * share), slots) == lax.div(column, batch_rows)
        real = lax.rem(lax.div(row, share), 2) == 0
        own, other = spread(own_ref), spread(other_ref)
        sign = (2 * core - 1).astype(F32)
        own_out[...] = jnp.where(keep, jnp.where(real, own, sign * other), 0.0).astype(BF16)
        other_out[...] = jnp.where(keep, jnp.where(real, other, -sign * own), 0.0).astype(BF16)

    shape = jax.ShapeDtypeStruct((high, slots * batch_rows), BF16)
    return pl.pallas_call(
        body,
        out_shape=[shape, shape],
        in_specs=[pl.BlockSpec(memory_space=pltpu.SMEM)] + vmem(2),
        out_specs=vmem(2),
        compiler_params=PARAMS,
        name="weights",
    )(where, own_batch, other_batch)


def second_product(own_weights, other_weights, blocks):
    high, rows = own_weights.shape
    half = high // 2
    width = blocks[0][0].shape[1]
    flat = []
    for pair_block, _, single in blocks:
        flat += [pair_block, single]

    def body(own_ref, other_ref, *refs):
        block_refs, (mine, theirs) = refs[: len(flat)], refs[len(flat):]
        for number, (_, place, _) in enumerate(blocks):
            first, later = block_refs[2 * number], block_refs[2 * number + 1]
            both = jnp.dot(
                own_ref[...], first[place * rows:(place + 1) * rows, :], preferred_element_type=F32
            ) + jnp.dot(other_ref[...], later[...], preferred_element_type=F32)
            both = both.astype(BF16)
            mine[number * half:(number + 1) * half, :] = both[:half]
            theirs[number * half:(number + 1) * half, :] = both[half:]

    shape = jax.ShapeDtypeStruct((len(blocks) * half, width), BF16)
    return pl.pallas_call(
        body,
        out_shape=[shape, shape],
        in_specs=vmem(2 + len(flat)),
        out_specs=vmem(2),
        compiler_params=PARAMS,
        name="second_product",
    )(own_weights, other_weights, *flat)


def place_pairs(order, pair_column, pieces, share):
    width = pieces[0].shape[1]
    slots = order.shape[0]
    each = 2 * share

    def body(order_ref, pair_ref, *refs):
        piece_refs, out_ref, held = refs[: len(pieces)], refs[-2], refs[-1]
        start = 0
        for ref in piece_refs:
            for tile in range(width // LANES):
                held[tile, start:start + ref.shape[0], :] = ref[:, tile * LANES:(tile + 1) * LANES].astype(F32)
            start += ref.shape[0]
        lane = lax.broadcasted_iota(jnp.int32, (slots, slots), 1)
        ordered = (order_ref[...] == lane).astype(F32).astype(BF16)
        paired = (pair_ref[...] == lane).astype(F32).astype(BF16)
        place = jnp.dot(ordered, paired, preferred_element_type=F32).astype(BF16)
        for number in range(each):
            for tile in range(width // LANES):
                rows = held[tile, pl.ds(number, slots, stride=each), :].astype(BF16)
                placed = lax.dot_general(rows, place, (((0,), (0,)), ((), ())), preferred_element_type=F32)
                lanes = pl.ds(tile * LANES, LANES)
                out_ref[number // share, number % share, lanes, :] = placed.astype(BF16)

    return pl.pallas_call(
        body,
        out_shape=jax.ShapeDtypeStruct((2, share, width, slots), BF16),
        in_specs=vmem(2 + len(pieces)),
        out_specs=pl.BlockSpec(memory_space=pltpu.VMEM),
        scratch_shapes=[pltpu.VMEM((width // LANES, slots * each, LANES), F32)],
        compiler_params=PARAMS,
        name="place_pairs",
    )(order, pair_column, *pieces)


def on_device(n_coef, n_pair, integrals, coefficients, shell_starts, pair_ids):
    grid = Grid(n_pair)
    swap = functools.partial(lax.ppermute, axis_name="pair", perm=grid.across_core())
    slots, batch_rows, ao_width = integrals.shape
    occupied = coefficients.shape[2]
    share = occupied // n_pair
    rows = slots * batch_rows
    depth = ao_width // n_pair
    piece = depth // n_coef

    me = lax.axis_index("pair")
    core, x, y, z = me % 2, me // 2 % 2, me // 4 % 2, me // 8
    q = jnp.where(x == 0, z, grid.ring - 1 - z)

    def source_of(offset, flip, on_core, rows_core):
        spot = (q + jnp.where(on_core == 0, offset, -offset) + grid.ring) % grid.ring
        return grid.device(spot, (y + flip) % 2, rows_core)

    batch_index = (shell_starts[:, None] + jnp.arange(SHW, dtype=jnp.int32)[None, :]).reshape(-1)
    flat_ints = integrals.reshape(rows, ao_width)
    if n_coef > 1:
        coefficients = lax.all_gather(coefficients, "coef", axis=1, tiled=True)
        flat_ints = flat_ints.reshape(rows, n_coef, n_pair, piece).transpose(0, 2, 1, 3).reshape(rows, ao_width)
        batch_index = (
            batch_index // piece % n_pair * depth + batch_index // (n_pair * piece) * piece + batch_index % piece
        )
    batch_column = batch_index[:, None]

    own_rows = lax.dynamic_index_in_dim(coefficients, core, 0, keepdims=False)
    other_rows = swap(lax.dynamic_index_in_dim(coefficients, 1 - core, 0, keepdims=False))
    other_ints = swap(flat_ints)
    offsets = grid.offsets()
    groups = [offsets[:3], offsets[3:5], offsets[5:]] if len(offsets) > 5 else [offsets]

    pairs, singles, mirrored = gather_chips(grid, own_rows, other_rows)
    sources, total = [], None
    for number, group in enumerate(groups):
        parts = []
        for offset in group:
            for block, ids in (
                (pairs[offset], [(0, core), (1, core)]),
                (singles[offset], [(0, 1 - core)]),
                (mirrored[offset], [(1, 1 - core)]),
            ):
                named = [len(sources) + k for k in range(len(ids))]
                sources += [source_of(offset, flip, core, rows_core) for flip, rows_core in ids]
                parts.append((block, named))
        last = number == len(groups) - 1
        total = (total, parts, last)
        groups[number] = (group, parts, last)
    source = jnp.stack(sources).astype(jnp.int32)
    total = None
    for group, parts, last in groups:
        result = first_product(source, flat_ints, other_ints, batch_column, total, parts, last)
        total = result[0]
    half_own, leaving = result
    arrived = swap(leaving)
    half_other, other_batch = arrived[:rows], arrived[rows:]
    own_batch = leaving[rows:]

    own_weights, other_weights = weights(me[None].astype(jnp.int32), own_batch, other_batch, slots, share)
    pairs, singles, mirrored = gather_chips(grid, half_own, half_other)
    mine, theirs, mine_order, their_order = [], [], [], []
    within = jnp.arange(slots, dtype=jnp.int32)
    for group, _, _ in groups:
        blocks = []
        for offset in group:
            blocks += [(pairs[offset], 0, singles[offset]), (pairs[offset], 1, mirrored[offset])]
            for flip in range(2):
                mine_order.append(source_of(offset, flip, core, core) * slots + within)
                their_order.append(source_of(offset, flip, 1 - core, 1 - core) * slots + within)
        stay, leave = second_product(own_weights, other_weights, blocks)
        mine.append(stay)
        theirs.append(swap(leave))
    order = jnp.concatenate(mine_order + their_order)[:, None]
    return place_pairs(order, pair_ids.reshape(-1)[:, None], mine + theirs, share)


def solution(mesh):
    return jax.shard_map(
        functools.partial(on_device, mesh.shape["coef"], mesh.shape["pair"]),
        mesh=mesh,
        in_specs=(
            P(("coef", "pair"), None, None),
            P(None, ("coef", "pair"), None),
            P(),
            P("coef", None),
        ),
        out_specs=P(None, "pair", None, "coef"),
        check_vma=False,
    )
```

```python
import functools

import jax
import jax.numpy as jnp
from jax import lax
from jax.experimental import pallas as pl
from jax.experimental.pallas import tpu as pltpu
from jax.sharding import PartitionSpec as P

SHW = 4
LANES = 128
F32, BF16 = jnp.float32, jnp.bfloat16
VMEM_LIMIT = 40 * 1024 * 1024


class Grid:
    def __init__(self, n_pair):
        assert n_pair % 8 == 0
        self.nz = n_pair // 8
        self.ring = 2 * self.nz

    def device(self, spot, side, core):
        turned = (spot >= self.nz) * 1
        z = spot + turned * (self.ring - 1 - 2 * spot)
        x = turned + core * (side - turned)
        y = side + core * (turned - side)
        return ((z * 2 + y) * 2 + x) * 2 + core

    def place(self, device):
        core, x, y, z = device % 2, device // 2 % 2, device // 4 % 2, device // 8
        turned = x + core * (y - x)
        side = y + core * (x - y)
        return z + turned * (self.ring - 1 - 2 * z), side, core

    def moves(self, target):
        every = range(self.ring * 4)
        return [(device, int(self.device(*target(*self.place(device))))) for device in every]

    def around(self, way):
        return self.moves(lambda spot, side, core: ((spot + way * (1 - 2 * core)) % self.ring, side, core))

    def across(self):
        return self.moves(lambda spot, side, core: (spot, 1 - side, core))

    def across_core(self):
        return [(device, device ^ 1) for device in range(self.ring * 4)]

    def source(self, me, offset, flip):
        spot, side, core = self.place(me)
        spot = (spot + offset * (1 - 2 * core) + self.ring) % self.ring
        return self.device(spot, (side + flip) % 2, core)

    def groups(self):
        steps = [[-step, step] for step in range(1, self.nz)]
        return [[0] + steps[0]] + steps[1:] + [[-self.nz]] if steps else [[0, -self.nz]]


def gather_chips(grid, own):
    send = functools.partial(lax.ppermute, axis_name="pair")
    around = {-1: grid.around(1), 1: grid.around(-1)}
    across = grid.across()
    held = {0: own}
    for step in range(1, grid.nz + 1):
        for way in (-1, 1):
            if way == -1 or step < grid.nz:
                held[way * step] = send(held[way * (step - 1)], perm=around[way])
    return {offset: (block, send(block, perm=across)) for offset, block in held.items()}


def vmem(count):
    return [pl.BlockSpec(memory_space=pltpu.VMEM)] * count


PARAMS = pltpu.CompilerParams(vmem_limit_bytes=VMEM_LIMIT)


def first_product(source, own_ints, other_ints, batch_column, total, blocks):
    parts, depth, width = blocks[0].shape
    batch_rows = batch_column.shape[0]
    high = own_ints.shape[0] + other_ints.shape[0] + batch_rows
    begins = total is None

    def body(source_ref, own_ref, other_ref, batch_ref, *refs):
        block_refs, out_ref = refs[-1 - len(blocks):-1], refs[-1]
        for number, ref in enumerate(block_refs):
            start = pl.multiple_of(source_ref[number] * depth, depth)
            columns = pl.ds(start, depth)
            position = lax.broadcasted_iota(jnp.int32, (batch_rows, depth), 1) + start
            picks = (batch_ref[...] == position).astype(F32).astype(BF16)
            left = jnp.concatenate([own_ref[:, columns], other_ref[:, columns], picks], axis=0)
            for part in range(parts):
                term = jnp.dot(left, ref[part], preferred_element_type=F32)
                lanes = pl.ds(part * width, width)
                if number > 0:
                    out_ref[:, lanes] += term
                elif begins:
                    out_ref[:, lanes] = term
                else:
                    out_ref[:, lanes] = refs[0][:, lanes] + term

    operands = ([] if begins else [total]) + blocks
    return pl.pallas_call(
        body,
        out_shape=jax.ShapeDtypeStruct((high, parts * width), F32),
        in_specs=[pl.BlockSpec(memory_space=pltpu.SMEM)] + vmem(3 + len(operands)),
        out_specs=pl.BlockSpec(memory_space=pltpu.VMEM),
        compiler_params=PARAMS,
        name="first_product",
    )(source, own_ints, other_ints, batch_column, *operands)


def add_halves(kept, arrived, rows, width):
    batch_rows = kept.shape[0] - rows

    def body(kept_ref, arrived_ref, half_ref, batch_ref):
        for part in range(2):
            lanes = pl.ds(part * width, width)
            both = (kept_ref[:, lanes] + arrived_ref[:, lanes]).astype(BF16)
            half_ref[part * rows:(part + 1) * rows, :] = both[:rows]
            batch_ref[part * batch_rows:(part + 1) * batch_rows, :] = both[rows:]

    return pl.pallas_call(
        body,
        out_shape=[jax.ShapeDtypeStruct((2 * n, width), BF16) for n in (rows, batch_rows)],
        in_specs=vmem(2),
        out_specs=vmem(2),
        compiler_params=PARAMS,
        name="add_halves",
    )(kept, arrived)


def weights(where, batch, slots, share):
    batch_rows, width = batch.shape[0] // 2, batch.shape[1]
    high = 2 * slots * 2 * share
    deep = slots * batch_rows

    def body(where_ref, batch_ref, out_ref):
        me = where_ref[0]
        core = lax.rem(me, 2)
        row = lax.broadcasted_iota(jnp.int32, (high, width), 0)
        column = lax.broadcasted_iota(jnp.int32, (high, width), 1)
        half = lax.div(row, high // 2)
        wanted = (me - core + lax.rem(core + half, 2)) * share + lax.rem(row, share)
        chosen = (column == wanted).astype(F32).astype(BF16)
        repeat = (
            lax.broadcasted_iota(jnp.int32, (batch_rows, deep), 0)
            == lax.rem(lax.broadcasted_iota(jnp.int32, (batch_rows, deep), 1), batch_rows)
        ).astype(F32).astype(BF16)

        def spread(part):
            rows = batch_ref[part * batch_rows:(part + 1) * batch_rows, :]
            picked = lax.dot_general(chosen, rows, (((1,), (1,)), ((), ())), preferred_element_type=F32)
            return jnp.dot(picked.astype(BF16), repeat, preferred_element_type=F32)

        row = lax.broadcasted_iota(jnp.int32, (high, deep), 0)
        column = lax.broadcasted_iota(jnp.int32, (high, deep), 1)
        keep = lax.rem(lax.div(row, 2 * share), slots) == lax.div(column, batch_rows)
        real = lax.rem(lax.div(row, share), 2) == 0
        re, im = spread(0), spread(1)
        out_ref[:, :deep] = jnp.where(keep, jnp.where(real, re, -im), 0.0).astype(BF16)
        out_ref[:, deep:] = jnp.where(keep, jnp.where(real, im, re), 0.0).astype(BF16)

    return pl.pallas_call(
        body,
        out_shape=jax.ShapeDtypeStruct((high, 2 * deep), BF16),
        in_specs=[pl.BlockSpec(memory_space=pltpu.SMEM)] + vmem(1),
        out_specs=pl.BlockSpec(memory_space=pltpu.VMEM),
        compiler_params=PARAMS,
        name="weights",
    )(where, batch)


def second_product(matrix, blocks):
    half = matrix.shape[0] // 2
    width = blocks[0].shape[1]

    def body(matrix_ref, *refs):
        block_refs, (mine, theirs) = refs[: len(blocks)], refs[len(blocks):]
        for number, ref in enumerate(block_refs):
            both = jnp.dot(matrix_ref[...], ref[...], preferred_element_type=F32).astype(BF16)
            mine[number * half:(number + 1) * half, :] = both[:half]
            theirs[number * half:(number + 1) * half, :] = both[half:]

    shape = jax.ShapeDtypeStruct((len(blocks) * half, width), BF16)
    return pl.pallas_call(
        body,
        out_shape=[shape, shape],
        in_specs=vmem(1 + len(blocks)),
        out_specs=vmem(2),
        compiler_params=PARAMS,
        name="second_product",
    )(matrix, *blocks)


def place_pairs(order, pair_column, pieces, share):
    width = pieces[0].shape[1]
    slots = order.shape[0]
    each = 2 * share

    def body(order_ref, pair_ref, *refs):
        piece_refs, out_ref, held = refs[: len(pieces)], refs[-2], refs[-1]
        start = 0
        for ref in piece_refs:
            for tile in range(width // LANES):
                held[tile, start:start + ref.shape[0], :] = ref[:, tile * LANES:(tile + 1) * LANES].astype(F32)
            start += ref.shape[0]
        lane = lax.broadcasted_iota(jnp.int32, (slots, slots), 1)
        ordered = (order_ref[...] == lane).astype(F32).astype(BF16)
        paired = (pair_ref[...] == lane).astype(F32).astype(BF16)
        place = jnp.dot(ordered, paired, preferred_element_type=F32).astype(BF16)
        for number in range(each):
            for tile in range(width // LANES):
                rows = held[tile, pl.ds(number, slots, stride=each), :].astype(BF16)
                placed = lax.dot_general(rows, place, (((0,), (0,)), ((), ())), preferred_element_type=F32)
                lanes = pl.ds(tile * LANES, LANES)
                out_ref[number // share, number % share, lanes, :] = placed.astype(BF16)

    return pl.pallas_call(
        body,
        out_shape=jax.ShapeDtypeStruct((2, share, width, slots), BF16),
        in_specs=vmem(2 + len(pieces)),
        out_specs=pl.BlockSpec(memory_space=pltpu.VMEM),
        scratch_shapes=[pltpu.VMEM((width // LANES, slots * each, LANES), F32)],
        compiler_params=PARAMS,
        name="place_pairs",
    )(order, pair_column, *pieces)


def on_device(n_coef, n_pair, integrals, coefficients, shell_starts, pair_ids):
    grid = Grid(n_pair)
    swap = functools.partial(lax.ppermute, axis_name="pair", perm=grid.across_core())
    slots, batch_rows, ao_width = integrals.shape
    occupied = coefficients.shape[2]
    share = occupied // n_pair
    rows = slots * batch_rows
    depth = ao_width // n_pair
    piece = depth // n_coef
    me = lax.axis_index("pair").astype(jnp.int32)

    batch_index = (shell_starts[:, None] + jnp.arange(SHW, dtype=jnp.int32)[None, :]).reshape(-1)
    flat_ints = integrals.reshape(rows, ao_width)
    if n_coef > 1:
        coefficients = lax.all_gather(coefficients, "coef", axis=1, tiled=True)
        flat_ints = flat_ints.reshape(rows, n_coef, n_pair, piece).transpose(0, 2, 1, 3).reshape(rows, ao_width)
        batch_index = (
            batch_index // piece % n_pair * depth + batch_index // (n_pair * piece) * piece + batch_index % piece
        )
    batch_column = batch_index[:, None]

    other_ints = swap(flat_ints)
    gathered = gather_chips(grid, coefficients)
    total = None
    for group in grid.groups():
        blocks = [block for offset in group for block in gathered[offset]]
        source = jnp.stack([grid.source(me, offset, flip) for offset in group for flip in range(2)])
        total = first_product(source, flat_ints, other_ints, batch_column, total, blocks)
    kept = jnp.concatenate([total[:rows], total[2 * rows:]], axis=0)
    half, batch = add_halves(kept, swap(total[rows:]), rows, occupied)
    matrix = weights(me[None], batch, slots, share)

    gathered = gather_chips(grid, half)
    mine, theirs, mine_order, their_order = [], [], [], []
    within = jnp.arange(slots, dtype=jnp.int32)
    for group in grid.groups():
        stay, leave = second_product(matrix, [block for offset in group for block in gathered[offset]])
        mine.append(stay)
        theirs.append(swap(leave))
        for offset in group:
            for flip in range(2):
                mine_order.append(grid.source(me, offset, flip) * slots + within)
                their_order.append(grid.source(me ^ 1, offset, flip) * slots + within)
    order = jnp.concatenate(mine_order + their_order)[:, None]
    return place_pairs(order, pair_ids.reshape(-1)[:, None], mine + theirs, share)


def solution(mesh):
    return jax.shard_map(
        functools.partial(on_device, mesh.shape["coef"], mesh.shape["pair"]),
        mesh=mesh,
        in_specs=(
            P(("coef", "pair"), None, None),
            P(None, ("coef", "pair"), None),
            P(),
            P("coef", None),
        ),
        out_specs=P(None, "pair", None, "coef"),
        check_vma=False,
    )
```

```python
import functools

import jax
import jax.numpy as jnp
from jax import lax
from jax.experimental import pallas as pl
from jax.experimental.pallas import tpu as pltpu
from jax.sharding import PartitionSpec as P

SHW = 4
LANES = 128
F32, BF16 = jnp.float32, jnp.bfloat16
VMEM_LIMIT = 16 * 1024 * 1024


class Grid:
    def __init__(self, n_pair):
        assert n_pair % 8 == 0
        self.nz = n_pair // 8
        self.ring = 2 * self.nz

    def device(self, spot, side, core):
        turned = (spot >= self.nz) * 1
        z = spot + turned * (self.ring - 1 - 2 * spot)
        x = turned + core * (side - turned)
        y = side + core * (turned - side)
        return ((z * 2 + y) * 2 + x) * 2 + core

    def place(self, device):
        core, x, y, z = device % 2, device // 2 % 2, device // 4 % 2, device // 8
        turned = x + core * (y - x)
        side = y + core * (x - y)
        return z + turned * (self.ring - 1 - 2 * z), side, core

    def moves(self, target):
        every = range(self.ring * 4)
        return [(device, int(self.device(*target(*self.place(device))))) for device in every]

    def around(self, way):
        return self.moves(lambda spot, side, core: ((spot + way * (1 - 2 * core)) % self.ring, side, core))

    def mate(self, device):
        return device + 1 - 2 * (device % 2)

    def opposite(self, device):
        spot, side, core = self.place(device)
        return self.device(spot, 1 - side, core)

    def helpers(self, device):
        return [device, self.mate(device), self.opposite(device), self.opposite(self.mate(device))]

    def helped(self, device):
        return [device, self.mate(device), self.opposite(device), self.mate(self.opposite(device))]

    def exchange(self, blocks, partners):
        every = range(self.ring * 4)
        return [
            lax.ppermute(block, "pair", [(device, int(partners(device)[k])) for device in every])
            for k, block in zip((1, 2, 3), blocks)
        ]

    def spot(self, device, offset):
        spot, _, core = self.place(device)
        return (spot + offset * (1 - 2 * core) + self.ring) % self.ring

    def source_at(self, device, spot):
        _, side, core = self.place(device)
        return self.device(spot, side, core)

    def source(self, device, offset):
        _, side, core = self.place(device)
        return self.device(self.spot(device, offset), side, core)


def gather_ring(grid, own):
    around = {-1: grid.around(1), 1: grid.around(-1)}
    held, groups = {0: own}, [[0]]
    for step in range(1, grid.nz + 1):
        ways = (-1, 1) if step < grid.nz else (-1,)
        for way in ways:
            held[way * step] = lax.ppermute(held[way * (step - 1)], "pair", around[way])
        groups.append([way * step for way in ways])
    return held, [groups[0] + groups[1]] + groups[2:]


def vmem(count):
    return [pl.BlockSpec(memory_space=pltpu.VMEM)] * count


PARAMS = pltpu.CompilerParams(vmem_limit_bytes=VMEM_LIMIT)


def share_integrals(columns, integrals, depth):
    rows = integrals.shape[0]
    partners, ring = columns.shape

    def body(columns_ref, ints_ref, *refs):
        outs, moved = refs[:-1], refs[-1]
        copies = []
        for k, out in enumerate(outs):
            for spot in range(ring):
                start = pl.multiple_of(columns_ref[k, spot] * depth, depth)
                copies.append(
                    pltpu.make_async_copy(
                        ints_ref.at[:, pl.ds(start, depth)], out.at[:, pl.ds(spot * depth, depth)], moved.at[k, spot]
                    )
                )
        for copy in copies:
            copy.start()
        for copy in copies:
            copy.wait()

    return pl.pallas_call(
        body,
        out_shape=[jax.ShapeDtypeStruct((rows, ring * depth), BF16)] * partners,
        in_specs=[pl.BlockSpec(memory_space=pltpu.SMEM), pl.BlockSpec(memory_space=pl.ANY)],
        out_specs=vmem(partners),
        scratch_shapes=[pltpu.SemaphoreType.DMA((partners, ring))],
        compiler_params=PARAMS,
        name="share_integrals",
    )(columns, integrals)


def first_product(spots, source, ints, batch_column, total, blocks, last):
    parts, depth, width = blocks[0].shape
    rows, batch_rows = ints[0].shape[0], batch_column.shape[0]
    high = len(ints) * rows + batch_rows
    begins = total is None

    def body(spots_ref, source_ref, batch_ref, *refs):
        ints_refs, refs = refs[: len(ints)], refs[len(ints):]
        total_ref, refs = (None, refs) if begins else (refs[0], refs[1:])
        block_refs, outs = refs[: len(blocks)], refs[len(blocks):]
        sum_ref = outs[-1]
        for number, ref in enumerate(block_refs):
            columns = pl.ds(pl.multiple_of(spots_ref[number] * depth, depth), depth)
            position = lax.broadcasted_iota(jnp.int32, (batch_rows, depth), 1) + source_ref[number] * depth
            picks = (batch_ref[...] == position).astype(F32).astype(BF16)
            left = jnp.concatenate([ints_ref[:, columns] for ints_ref in ints_refs] + [picks], axis=0)
            for part in range(parts):
                term = jnp.dot(left, ref[part], preferred_element_type=F32)
                lanes = pl.ds(part * width, width)
                if number > 0:
                    sum_ref[:, lanes] += term
                elif begins:
                    sum_ref[:, lanes] = term
                else:
                    sum_ref[:, lanes] = total_ref[:, lanes] + term
        if last:
            for k, out in enumerate(outs[:-1]):
                out[:rows, :] = sum_ref[k * rows:(k + 1) * rows, :].astype(out.dtype)
                out[rows:, :] = sum_ref[len(ints) * rows:, :].astype(out.dtype)

    totals = [] if begins else [total]
    whole = jax.ShapeDtypeStruct((high, parts * width), F32)
    kinds = (F32, F32, BF16, BF16)
    shapes = [jax.ShapeDtypeStruct((rows + batch_rows, parts * width), kind) for kind in kinds] if last else [whole]
    return pl.pallas_call(
        body,
        out_shape=shapes,
        in_specs=[pl.BlockSpec(memory_space=pltpu.SMEM)] * 2 + vmem(1 + len(ints) + len(totals) + len(blocks)),
        out_specs=vmem(len(shapes)),
        scratch_shapes=[pltpu.VMEM(whole.shape, F32)] if last else [],
        compiler_params=PARAMS,
        cost_estimate=pl.CostEstimate(
            flops=10 * high * depth * width * parts * len(blocks), bytes_accessed=0, transcendentals=0
        ),
        name="first_product",
    )(spots, source, batch_column, *ints, *totals, *blocks)


def add_partners(sums, rows, width):
    batch_rows = sums[0].shape[0] - rows

    def body(*refs):
        half_ref, batch_ref = refs[-2:]
        for part in range(2):
            lanes = pl.ds(part * width, width)
            both = sum(ref[:, lanes].astype(F32) for ref in refs[:-2]).astype(BF16)
            half_ref[part * rows:(part + 1) * rows, :] = both[:rows]
            batch_ref[part * batch_rows:(part + 1) * batch_rows, :] = both[rows:]

    return pl.pallas_call(
        body,
        out_shape=[jax.ShapeDtypeStruct((2 * n, width), BF16) for n in (rows, batch_rows)],
        in_specs=vmem(len(sums)),
        out_specs=vmem(2),
        compiler_params=PARAMS,
        name="add_partners",
    )(*sums)


def weights(devices, batch, slots, share):
    batch_rows, width = batch.shape[0] // 2, batch.shape[1]
    partners = devices.shape[0]
    each = slots * 2 * share
    deep = slots * batch_rows

    def body(devices_ref, batch_ref, out_ref):
        repeat = (
            lax.broadcasted_iota(jnp.int32, (batch_rows, deep), 0)
            == lax.rem(lax.broadcasted_iota(jnp.int32, (batch_rows, deep), 1), batch_rows)
        ).astype(F32).astype(BF16)
        row = lax.broadcasted_iota(jnp.int32, (each, deep), 0)
        keep = lax.rem(lax.div(row, 2 * share), slots) == lax.div(
            lax.broadcasted_iota(jnp.int32, (each, deep), 1), batch_rows
        )
        real = lax.rem(lax.div(row, share), 2) == 0
        row = lax.broadcasted_iota(jnp.int32, (each, width), 0)
        column = lax.broadcasted_iota(jnp.int32, (each, width), 1)
        for k in range(partners):
            chosen = (column == devices_ref[k] * share + lax.rem(row, share)).astype(F32).astype(BF16)

            def spread(part):
                rows = batch_ref[part * batch_rows:(part + 1) * batch_rows, :]
                picked = lax.dot_general(chosen, rows, (((1,), (1,)), ((), ())), preferred_element_type=F32)
                return jnp.dot(picked.astype(BF16), repeat, preferred_element_type=F32)

            re, im = spread(0), spread(1)
            here = pl.ds(k * each, each)
            out_ref[here, :deep] = jnp.where(keep, jnp.where(real, re, -im), 0.0).astype(BF16)
            out_ref[here, deep:] = jnp.where(keep, jnp.where(real, im, re), 0.0).astype(BF16)

    return pl.pallas_call(
        body,
        out_shape=jax.ShapeDtypeStruct((partners * each, 2 * deep), BF16),
        in_specs=[pl.BlockSpec(memory_space=pltpu.SMEM)] + vmem(1),
        out_specs=pl.BlockSpec(memory_space=pltpu.VMEM),
        compiler_params=PARAMS,
        name="weights",
    )(devices, batch)


def second_product(matrix, blocks, partners):
    each = matrix.shape[0] // partners
    width = blocks[0].shape[1]

    def body(matrix_ref, *refs):
        block_refs, outs = refs[: len(blocks)], refs[len(blocks):]
        for number, ref in enumerate(block_refs):
            every = jnp.dot(matrix_ref[...], ref[...], preferred_element_type=F32).astype(BF16)
            for k, out in enumerate(outs):
                out[number * each:(number + 1) * each, :] = every[k * each:(k + 1) * each]

    return pl.pallas_call(
        body,
        out_shape=[jax.ShapeDtypeStruct((len(blocks) * each, width), BF16)] * partners,
        in_specs=vmem(1 + len(blocks)),
        out_specs=vmem(partners),
        compiler_params=PARAMS,
        name="second_product",
    )(matrix, *blocks)


def place_pairs(order, pair_column, pieces, share):
    width = pieces[0].shape[1]
    slots = order.shape[0]
    each = 2 * share

    def body(order_ref, pair_ref, *refs):
        piece_refs, out_ref, held = refs[: len(pieces)], refs[-2], refs[-1]
        start = 0
        for ref in piece_refs:
            for tile in range(width // LANES):
                held[tile, start:start + ref.shape[0], :] = ref[:, tile * LANES:(tile + 1) * LANES].astype(F32)
            start += ref.shape[0]
        lane = lax.broadcasted_iota(jnp.int32, (slots, slots), 1)
        ordered = (order_ref[...] == lane).astype(F32).astype(BF16)
        paired = (pair_ref[...] == lane).astype(F32).astype(BF16)
        place = jnp.dot(ordered, paired, preferred_element_type=F32).astype(BF16)
        for number in range(each):
            for tile in range(width // LANES):
                rows = held[tile, pl.ds(number, slots, stride=each), :].astype(BF16)
                placed = lax.dot_general(rows, place, (((0,), (0,)), ((), ())), preferred_element_type=F32)
                lanes = pl.ds(tile * LANES, LANES)
                out_ref[number // share, number % share, lanes, :] = placed.astype(BF16)

    return pl.pallas_call(
        body,
        out_shape=jax.ShapeDtypeStruct((2, share, width, slots), BF16),
        in_specs=vmem(2 + len(pieces)),
        out_specs=pl.BlockSpec(memory_space=pltpu.VMEM),
        scratch_shapes=[pltpu.VMEM((width // LANES, slots * each, LANES), F32)],
        compiler_params=PARAMS,
        name="place_pairs",
    )(order, pair_column, *pieces)


def on_device(n_coef, n_pair, integrals, coefficients, shell_starts, pair_ids):
    grid = Grid(n_pair)
    slots, batch_rows, ao_width = integrals.shape
    occupied = coefficients.shape[2]
    share = occupied // n_pair
    rows = slots * batch_rows
    depth = ao_width // n_pair
    piece = depth // n_coef
    me = lax.axis_index("pair").astype(jnp.int32)

    batch_index = (shell_starts[:, None] + jnp.arange(SHW, dtype=jnp.int32)[None, :]).reshape(-1)
    flat_ints = integrals.reshape(rows, ao_width)
    if n_coef > 1:
        coefficients = lax.all_gather(coefficients, "coef", axis=1, tiled=True)
        flat_ints = flat_ints.reshape(rows, n_coef, n_pair, piece).transpose(0, 2, 1, 3).reshape(rows, ao_width)
        batch_index = (
            batch_index // piece % n_pair * depth + batch_index // (n_pair * piece) * piece + batch_index % piece
        )
    batch_column = batch_index[:, None]

    helpers, helped = grid.helpers(me), grid.helped(me)
    columns = jnp.stack([grid.source_at(device, jnp.arange(grid.ring, dtype=jnp.int32)) for device in helpers])
    kept, *leaving = share_integrals(columns, flat_ints, depth)
    ints = [kept, *grid.exchange(leaving, grid.helpers)]
    held, groups = gather_ring(grid, coefficients)
    total = None
    for number, group in enumerate(groups):
        spots = jnp.stack([grid.spot(me, offset) for offset in group])
        source = jnp.stack([grid.source(me, offset) for offset in group])
        last = number == len(groups) - 1
        blocks = [held[offset] for offset in group]
        result = first_product(spots, source, ints, batch_column, total, blocks, last)
        total = result[0]
    kept, *leaving = result
    half, batch = add_partners([kept, *grid.exchange(leaving, grid.helped)], rows, occupied)
    matrix = weights(jnp.stack(helped), batch, slots, share)

    held, groups = gather_ring(grid, half)
    pieces, order = [], []
    within = jnp.arange(slots, dtype=jnp.int32)
    for group in groups:
        kept, *leaving = second_product(matrix, [held[offset] for offset in group], len(helped))
        pieces += [kept, *grid.exchange(leaving, grid.helped)]
        order += [grid.source(device, offset) * slots + within for device in helpers for offset in group]
    return place_pairs(jnp.concatenate(order)[:, None], pair_ids.reshape(-1)[:, None], pieces, share)


def solution(mesh):
    return jax.shard_map(
        functools.partial(on_device, mesh.shape["coef"], mesh.shape["pair"]),
        mesh=mesh,
        in_specs=(
            P(("coef", "pair"), None, None),
            P(None, ("coef", "pair"), None),
            P(),
            P("coef", None),
        ),
        out_specs=P(None, "pair", None, "coef"),
        check_vma=False,
    )
```

```python
import functools

import jax
import jax.numpy as jnp
from jax import lax
from jax.experimental import pallas as pl
from jax.experimental.pallas import tpu as pltpu
from jax.sharding import PartitionSpec as P

SHW = 4
LANES = 128
F32, BF16 = jnp.float32, jnp.bfloat16
VMEM_LIMIT = 16 * 1024 * 1024


class Grid:
    def __init__(self, n_pair):
        assert n_pair % 8 == 0
        self.nz = n_pair // 8
        self.ring = 2 * self.nz

    def device(self, spot, side, core):
        turned = (spot >= self.nz) * 1
        z = spot + turned * (self.ring - 1 - 2 * spot)
        x = turned + core * (side - turned)
        y = side + core * (turned - side)
        return ((z * 2 + y) * 2 + x) * 2 + core

    def place(self, device):
        core, x, y, z = device % 2, device // 2 % 2, device // 4 % 2, device // 8
        turned = x + core * (y - x)
        side = y + core * (x - y)
        return z + turned * (self.ring - 1 - 2 * z), side, core

    def moves(self, target):
        every = range(self.ring * 4)
        return [(device, int(self.device(*target(*self.place(device))))) for device in every]

    def around(self, way):
        return self.moves(lambda spot, side, core: ((spot + way * (1 - 2 * core)) % self.ring, side, core))

    def mate(self, device):
        return device + 1 - 2 * (device % 2)

    def opposite(self, device):
        spot, side, core = self.place(device)
        return self.device(spot, 1 - side, core)

    def helpers(self, device):
        return [device, self.mate(device), self.opposite(device), self.opposite(self.mate(device))]

    def helped(self, device):
        return [device, self.mate(device), self.opposite(device), self.mate(self.opposite(device))]

    def send(self, block, target):
        return lax.ppermute(block, "pair", [(device, int(target(device))) for device in range(self.ring * 4)])

    def exchange(self, blocks, partners):
        return [self.send(block, lambda device: partners(device)[k]) for k, block in zip((1, 2, 3), blocks)]

    def spot(self, device, offset):
        spot, _, core = self.place(device)
        return (spot + offset * (1 - 2 * core) + self.ring) % self.ring

    def source_at(self, device, spot):
        _, side, core = self.place(device)
        return self.device(spot, side, core)

    def source(self, device, offset):
        _, side, core = self.place(device)
        return self.device(self.spot(device, offset), side, core)


def after(value, *done):
    return lax.optimization_barrier((value, *done))[0] if done else value


def gather_ring(grid, own, meanwhile):
    around = {-1: grid.around(1), 1: grid.around(-1)}
    held, gates = {0: own}, [[]]
    for step in range(1, grid.nz + 1):
        ways = (-1, 1) if step < grid.nz else (-1,)
        for way in ways:
            block = after(held[way * (step - 1)], *gates[step - 1])
            held[way * step] = lax.ppermute(block, "pair", around[way])
        gates.append(meanwhile(held, [0] if step == 1 else [1 - step, step - 1]))
    meanwhile(held, [-grid.nz])
    return held


def vmem(count):
    return [pl.BlockSpec(memory_space=pltpu.VMEM)] * count


PARAMS = pltpu.CompilerParams(vmem_limit_bytes=VMEM_LIMIT)


def in_hbm(array):
    return pltpu.with_memory_space_constraint(array, pltpu.HBM)


def share_integrals(grid, where, integrals, depth):
    rows = integrals.shape[0]

    def body(where_ref, ints_ref, *refs):
        outs, moved = refs[:-1], refs[-1]
        copies = []
        for k, (out, helper) in enumerate(zip(outs, grid.helpers(where_ref[0]))):
            for spot in range(grid.ring):
                start = pl.multiple_of(grid.source_at(helper, spot) * depth, depth)
                copies.append(
                    pltpu.make_async_copy(
                        ints_ref.at[:, pl.ds(start, depth)], out.at[:, pl.ds(spot * depth, depth)], moved.at[k, spot]
                    )
                )
        for copy in copies:
            copy.start()
        for copy in copies:
            copy.wait()

    return pl.pallas_call(
        body,
        out_shape=[jax.ShapeDtypeStruct((rows, grid.ring * depth), BF16)] * 4,
        in_specs=[pl.BlockSpec(memory_space=pltpu.SMEM), pl.BlockSpec(memory_space=pl.ANY)],
        out_specs=vmem(4),
        scratch_shapes=[pltpu.SemaphoreType.DMA((4, grid.ring))],
        compiler_params=PARAMS,
        name="share_integrals",
    )(where, in_hbm(integrals))


def first_product(grid, where, offsets, ints, batch_column, total, blocks, last):
    parts, depth, width = blocks[0].shape
    rows, batch_rows = ints[0].shape[0], batch_column.shape[0]
    high = len(ints) * rows + batch_rows
    begins = total is None

    def body(where_ref, batch_ref, *refs):
        ints_refs, refs = refs[: len(ints)], refs[len(ints):]
        total_ref, refs = (None, refs) if begins else (refs[0], refs[1:])
        block_refs, outs = refs[: len(blocks)], refs[len(blocks):]
        sum_ref = outs[-1]
        me = where_ref[0]
        for number, (offset, ref) in enumerate(zip(offsets, block_refs)):
            columns = pl.ds(pl.multiple_of(grid.spot(me, offset) * depth, depth), depth)
            position = lax.broadcasted_iota(jnp.int32, (batch_rows, depth), 1) + grid.source(me, offset) * depth
            picks = (batch_ref[...] == position).astype(F32).astype(BF16)
            left = jnp.concatenate([ints_ref[:, columns] for ints_ref in ints_refs] + [picks], axis=0)
            for part in range(parts):
                term = jnp.dot(left, ref[part], preferred_element_type=F32)
                lanes = pl.ds(part * width, width)
                if number > 0:
                    sum_ref[:, lanes] += term
                elif begins:
                    sum_ref[:, lanes] = term
                else:
                    sum_ref[:, lanes] = total_ref[:, lanes] + term
        if last:
            for k, out in enumerate(outs[:-1]):
                out[:rows, :] = sum_ref[k * rows:(k + 1) * rows, :].astype(out.dtype)
                out[rows:, :] = sum_ref[len(ints) * rows:, :].astype(out.dtype)

    totals = [] if begins else [total]
    whole = jax.ShapeDtypeStruct((high, parts * width), F32)
    kinds = (F32, F32, BF16, BF16)
    shapes = [jax.ShapeDtypeStruct((rows + batch_rows, parts * width), kind) for kind in kinds] if last else [whole]
    return pl.pallas_call(
        body,
        out_shape=shapes,
        in_specs=[pl.BlockSpec(memory_space=pltpu.SMEM)] + vmem(1 + len(ints) + len(totals) + len(blocks)),
        out_specs=vmem(len(shapes)),
        scratch_shapes=[pltpu.VMEM(whole.shape, F32)] if last else [],
        compiler_params=PARAMS,
        cost_estimate=pl.CostEstimate(
            flops=10 * high * depth * width * parts * len(blocks), bytes_accessed=0, transcendentals=0
        ),
        name="first_product",
    )(where, batch_column, *ints, *totals, *blocks)


def add_partners(sums, rows, width):
    batch_rows = sums[0].shape[0] - rows

    def body(*refs):
        half_ref, batch_ref = refs[-2:]
        for part in range(2):
            lanes = pl.ds(part * width, width)
            both = sum(ref[:, lanes].astype(F32) for ref in refs[:-2]).astype(BF16)
            half_ref[part * rows:(part + 1) * rows, :] = both[:rows]
            batch_ref[part * batch_rows:(part + 1) * batch_rows, :] = both[rows:]

    return pl.pallas_call(
        body,
        out_shape=[jax.ShapeDtypeStruct((2 * n, width), BF16) for n in (rows, batch_rows)],
        in_specs=vmem(len(sums)),
        out_specs=vmem(2),
        compiler_params=PARAMS,
        name="add_partners",
    )(*sums)


def weights(grid, where, batch, slots, share):
    batch_rows, width = batch.shape[0] // 2, batch.shape[1]
    each = slots * 2 * share
    deep = slots * batch_rows

    def body(where_ref, batch_ref, out_ref):
        repeat = (
            lax.broadcasted_iota(jnp.int32, (batch_rows, deep), 0)
            == lax.rem(lax.broadcasted_iota(jnp.int32, (batch_rows, deep), 1), batch_rows)
        ).astype(F32).astype(BF16)
        row = lax.broadcasted_iota(jnp.int32, (each, deep), 0)
        keep = lax.rem(lax.div(row, 2 * share), slots) == lax.div(
            lax.broadcasted_iota(jnp.int32, (each, deep), 1), batch_rows
        )
        real = lax.rem(lax.div(row, share), 2) == 0
        row = lax.broadcasted_iota(jnp.int32, (each, width), 0)
        column = lax.broadcasted_iota(jnp.int32, (each, width), 1)
        for k, device in enumerate(grid.helped(where_ref[0])):
            chosen = (column == device * share + lax.rem(row, share)).astype(F32).astype(BF16)

            def spread(part):
                rows = batch_ref[part * batch_rows:(part + 1) * batch_rows, :]
                picked = lax.dot_general(chosen, rows, (((1,), (1,)), ((), ())), preferred_element_type=F32)
                return jnp.dot(picked.astype(BF16), repeat, preferred_element_type=F32)

            re, im = spread(0), spread(1)
            here = pl.ds(k * each, each)
            out_ref[here, :deep] = jnp.where(keep, jnp.where(real, re, -im), 0.0).astype(BF16)
            out_ref[here, deep:] = jnp.where(keep, jnp.where(real, im, re), 0.0).astype(BF16)

    return pl.pallas_call(
        body,
        out_shape=jax.ShapeDtypeStruct((4 * each, 2 * deep), BF16),
        in_specs=[pl.BlockSpec(memory_space=pltpu.SMEM)] + vmem(1),
        out_specs=pl.BlockSpec(memory_space=pltpu.VMEM),
        compiler_params=PARAMS,
        name="weights",
    )(where, batch)


def second_product(matrix, blocks):
    each = matrix.shape[0] // 4
    width = blocks[0].shape[1]

    def body(matrix_ref, *refs):
        block_refs, outs = refs[: len(blocks)], refs[len(blocks):]
        high = len(blocks) * each
        for number, ref in enumerate(block_refs):
            every = jnp.dot(matrix_ref[...], ref[...], preferred_element_type=F32).astype(BF16)
            for k, (out, start) in enumerate(zip((outs[0], outs[1], outs[2], outs[2]), (0, 0, 0, high))):
                start += number * each
                out[start:start + each, :] = every[k * each:(k + 1) * each]

    return pl.pallas_call(
        body,
        out_shape=[jax.ShapeDtypeStruct((n * len(blocks) * each, width), BF16) for n in (1, 1, 2)],
        in_specs=vmem(1 + len(blocks)),
        out_specs=vmem(3),
        compiler_params=PARAMS,
        name="second_product",
    )(matrix, *blocks)


def place_pairs(grid, where, groups, pair_row, pieces, share):
    width = pieces[0].shape[1]
    pairs = pair_row.shape[1]
    each = 2 * share
    slots = pairs // (4 * grid.ring)

    def body(where_ref, pair_ref, *refs):
        piece_refs, (out_ref, held, ready, leaves) = refs[: len(pieces)], refs[-4:]
        start = 0
        for number, ref in enumerate(piece_refs):
            rows = len(groups[number // 4]) * slots * each
            for tile in range(width // LANES):
                held[tile, start:start + rows, :] = ref[:rows, tile * LANES:(tile + 1) * LANES].astype(F32)
            start += rows
        row = lax.broadcasted_iota(jnp.int32, (pairs, pairs), 0)
        lane = lax.broadcasted_iota(jnp.int32, (pairs, pairs), 1)
        helpers = grid.helpers(where_ref[0])
        sources = [grid.source(helper, offset) for group in groups for helper in helpers for offset in group]
        order = lax.rem(row, slots)
        for number, source in enumerate(sources):
            order += jnp.where(lax.div(row, slots) == number, source * slots, 0)
        ordered = (order == lane).astype(F32).astype(BF16)
        paired = (pair_ref[...] == row).astype(F32).astype(BF16)
        place = lax.dot_general(ordered, paired, (((1,), (1,)), ((), ())), preferred_element_type=F32).astype(BF16)
        copies = []
        for number in range(each):
            for tile in range(width // LANES):
                rows = held[tile, pl.ds(number, pairs, stride=each), :].astype(BF16)
                placed = lax.dot_general(rows, place, (((0,), (0,)), ((), ())), preferred_element_type=F32)
                ready[number, tile * LANES:(tile + 1) * LANES, :] = placed.astype(BF16)
            copies.append(
                pltpu.make_async_copy(ready.at[number], out_ref.at[number // share, number % share], leaves.at[number])
            )
            copies[-1].start()
        for copy in copies:
            copy.wait()

    return pl.pallas_call(
        body,
        out_shape=jax.ShapeDtypeStruct((2, share, width, pairs), BF16),
        in_specs=[pl.BlockSpec(memory_space=pltpu.SMEM)] + vmem(1 + len(pieces)),
        out_specs=pl.BlockSpec(memory_space=pl.ANY),
        scratch_shapes=[
            pltpu.VMEM((width // LANES, pairs * each, LANES), F32),
            pltpu.VMEM((each, width, pairs), BF16),
            pltpu.SemaphoreType.DMA((each,)),
        ],
        compiler_params=PARAMS,
        name="place_pairs",
    )(where, pair_row, *pieces)


def on_device(n_coef, n_pair, integrals, coefficients, shell_starts, pair_ids):
    grid = Grid(n_pair)
    slots, batch_rows, ao_width = integrals.shape
    occupied = coefficients.shape[2]
    share = occupied // n_pair
    rows = slots * batch_rows
    depth = ao_width // n_pair
    piece = depth // n_coef
    where = lax.axis_index("pair").astype(jnp.int32)[None]

    batch_index = (shell_starts[:, None] + jnp.arange(SHW, dtype=jnp.int32)[None, :]).reshape(-1)
    flat_ints = integrals.reshape(rows, ao_width)
    if n_coef > 1:
        coefficients = lax.all_gather(coefficients, "coef", axis=1, tiled=True)
        flat_ints = flat_ints.reshape(rows, n_coef, n_pair, piece).transpose(0, 2, 1, 3).reshape(rows, ao_width)
        batch_index = (
            batch_index // piece % n_pair * depth + batch_index // (n_pair * piece) * piece + batch_index % piece
        )
    batch_column = batch_index[:, None]

    kept, *leaving = share_integrals(grid, where, flat_ints, depth)
    ints = [kept, *grid.exchange(leaving, grid.helpers)]
    result = [None]

    def multiply(held, offsets):
        nonlocal result
        if offsets == [0] and grid.nz > 1:
            return [kept]
        group = [0, *offsets] if offsets == [-1, 1] else offsets
        blocks = [held[offset] for offset in group]
        last = offsets == [-grid.nz]
        result = first_product(grid, where, group, ints, batch_column, result[0], blocks, last)
        return ints if offsets == [-1, 1] else []

    gather_ring(grid, coefficients, multiply)
    kept, *leaving = result
    half, batch = add_partners([kept, *grid.exchange(leaving, grid.helped)], rows, occupied)
    matrix = weights(grid, where, batch, slots, share)
    pieces, groups = [], []
    before = []

    def transform(held, group):
        kept, aside, across = second_product(matrix, [held[offset] for offset in group])
        across = grid.send(across, grid.opposite)
        passed_on = across[kept.shape[0]:]
        arrived = [kept, grid.send(aside, grid.mate), across, grid.send(passed_on, grid.mate)]
        pieces.extend(arrived)
        groups.append(group)
        nonlocal before
        before, ready = arrived, before
        return [kept,*ready[:3]]

    gather_ring(grid, half, transform)
    return place_pairs(grid, where, groups, pair_ids, pieces, share)


def solution(mesh):
    return jax.shard_map(
        functools.partial(on_device, mesh.shape["coef"], mesh.shape["pair"]),
        mesh=mesh,
        in_specs=(
            P(("coef", "pair"), None, None),
            P(None, ("coef", "pair"), None),
            P(),
            P("coef", None),
        ),
        out_specs=P(None, "pair", None, "coef"),
        check_vma=False,
    )
```

```python
import functools

import jax
import jax.numpy as jnp
from jax import lax
from jax.experimental import pallas as pl
from jax.experimental.pallas import tpu as pltpu
from jax.sharding import PartitionSpec as P

SHW = 4
LANES = 128
F32, BF16 = jnp.float32, jnp.bfloat16
VMEM_LIMIT = 16 * 1024 * 1024


class Grid:
    def __init__(self, n_pair):
        assert n_pair % 8 == 0
        self.nz = n_pair // 8
        self.ring = 2 * self.nz

    def device(self, spot, side, core):
        turned = (spot >= self.nz) * 1
        z = spot + turned * (self.ring - 1 - 2 * spot)
        x = turned + core * (side - turned)
        y = side + core * (turned - side)
        return ((z * 2 + y) * 2 + x) * 2 + core

    def place(self, device):
        core, x, y, z = device % 2, device // 2 % 2, device // 4 % 2, device // 8
        turned = x + core * (y - x)
        side = y + core * (x - y)
        return z + turned * (self.ring - 1 - 2 * z), side, core

    def moves(self, target):
        every = range(self.ring * 4)
        return [(device, int(self.device(*target(*self.place(device))))) for device in every]

    def sense(self, side, core):
        return (1 - 2 * core) * (1 - 2 * side)

    def around(self, way):
        return self.moves(lambda spot, side, core: ((spot + way * self.sense(side, core)) % self.ring, side, core))

    def mate(self, device):
        return device + 1 - 2 * (device % 2)

    def opposite(self, device):
        spot, side, core = self.place(device)
        return self.device(spot, 1 - side, core)

    def helpers(self, device):
        return [device, self.mate(device), self.opposite(device), self.opposite(self.mate(device))]

    def helped(self, device):
        return [device, self.mate(device), self.opposite(device), self.mate(self.opposite(device))]

    def send(self, block, target):
        return lax.ppermute(block, "pair", [(device, int(target(device))) for device in range(self.ring * 4)])

    def exchange(self, blocks, partners):
        return [self.send(block, lambda device: partners(device)[k]) for k, block in zip((1, 2, 3), blocks)]

    def spot(self, device, offset):
        spot, side, core = self.place(device)
        return (spot + offset * self.sense(side, core) + self.ring) % self.ring

    def source_at(self, device, spot):
        _, side, core = self.place(device)
        return self.device(spot, side, core)

    def source(self, device, offset):
        _, side, core = self.place(device)
        return self.device(self.spot(device, offset), side, core)


def after(value, *done):
    return lax.optimization_barrier((value, *done))[0] if done else value


def gather_ring(grid, own, meanwhile):
    around = {-1: grid.around(1), 1: grid.around(-1)}
    held, gates = {0: own}, [[]]
    for step in range(1, grid.nz + 1):
        ways = (-1, 1) if step < grid.nz else (-1,)
        for way in ways:
            block = after(held[way * (step - 1)], *gates[step - 1])
            held[way * step] = lax.ppermute(block, "pair", around[way])
        gates.append(meanwhile(held, [0] if step == 1 else [1 - step, step - 1]))
    meanwhile(held, [-grid.nz])
    return held


def vmem(count):
    return [pl.BlockSpec(memory_space=pltpu.VMEM)] * count


PARAMS = pltpu.CompilerParams(vmem_limit_bytes=VMEM_LIMIT)


def in_hbm(array):
    return pltpu.with_memory_space_constraint(array, pltpu.HBM)


def share_integrals(grid, where, integrals, depth, groups):
    rows = integrals.shape[0]

    def body(where_ref, ints_ref, *refs):
        outs, moved = refs[:-1], refs[-1]
        copies = []
        for k, helper in enumerate(grid.helpers(where_ref[0])):
            for number, group in enumerate(groups):
                for place, offset in enumerate(group):
                    start = pl.multiple_of(grid.source(helper, offset) * depth, depth)
                    out = outs[4 * number + k].at[:, pl.ds(place * depth, depth)]
                    copies.append(
                        pltpu.make_async_copy(ints_ref.at[:, pl.ds(start, depth)], out, moved.at[len(copies)])
                    )
        for copy in copies:
            copy.start()
        for copy in copies:
            copy.wait()

    outs = pl.pallas_call(
        body,
        out_shape=[jax.ShapeDtypeStruct((rows, len(group) * depth), BF16) for group in groups for _ in range(4)],
        in_specs=[pl.BlockSpec(memory_space=pltpu.SMEM), pl.BlockSpec(memory_space=pl.ANY)],
        out_specs=vmem(4 * len(groups)),
        scratch_shapes=[pltpu.SemaphoreType.DMA((4 * grid.ring,))],
        compiler_params=PARAMS,
        name="share_integrals",
    )(where, in_hbm(integrals))
    return [outs[4 * number:4 * number + 4] for number in range(len(groups))]


def first_product(grid, where, offsets, ints, begin, batch_starts, moved_to, total, blocks, last):
    parts, depth, width = blocks[0].shape
    rows, batch_rows = ints[0].shape[0], batch_starts.shape[0] * SHW
    high = len(ints) * rows + batch_rows
    begins = total is None

    def body(where_ref, starts_ref, *refs):
        ints_refs, refs = refs[: len(ints)], refs[len(ints):]
        total_ref, refs = (None, refs) if begins else (refs[0], refs[1:])
        block_refs, outs = refs[: len(blocks)], refs[len(blocks):]
        sum_ref = outs[-1]
        me = where_ref[0]
        row = lax.broadcasted_iota(jnp.int32, (batch_rows, depth), 0)
        wanted = row
        for shell in range(batch_starts.shape[0]):
            wanted = jnp.where(row >= shell * SHW, row + (moved_to(starts_ref[shell]) - shell * SHW), wanted)
        for number, (offset, ref) in enumerate(zip(offsets, block_refs)):
            columns = pl.ds((begin + number) * depth, depth)
            position = lax.broadcasted_iota(jnp.int32, (batch_rows, depth), 1) + grid.source(me, offset) * depth
            picks = (wanted == position).astype(F32).astype(BF16)
            left = jnp.concatenate([ints_ref[:, columns] for ints_ref in ints_refs] + [picks], axis=0)
            for part in range(parts):
                term = jnp.dot(left, ref[part], preferred_element_type=F32)
                lanes = pl.ds(part * width, width)
                if number > 0:
                    sum_ref[:, lanes] += term
                elif begins:
                    sum_ref[:, lanes] = term
                else:
                    sum_ref[:, lanes] = total_ref[:, lanes] + term
        if last:
            for k, out in enumerate(outs[:-1]):
                out[:rows, :] = sum_ref[k * rows:(k + 1) * rows, :].astype(out.dtype)
                out[rows:, :] = sum_ref[len(ints) * rows:, :].astype(out.dtype)

    totals = [] if begins else [total]
    whole = jax.ShapeDtypeStruct((high, parts * width), F32)
    kinds = (F32, F32, BF16, BF16)
    shapes = [jax.ShapeDtypeStruct((rows + batch_rows, parts * width), kind) for kind in kinds] if last else [whole]
    return pl.pallas_call(
        body,
        out_shape=shapes,
        in_specs=[pl.BlockSpec(memory_space=pltpu.SMEM)] * 2 + vmem(len(ints) + len(totals) + len(blocks)),
        out_specs=vmem(len(shapes)),
        scratch_shapes=[pltpu.VMEM(whole.shape, F32)] if last else [],
        compiler_params=PARAMS,
        cost_estimate=pl.CostEstimate(
            flops=10 * high * depth * width * parts * len(blocks), bytes_accessed=0, transcendentals=0
        ),
        name="first_product",
    )(where, batch_starts, *ints, *totals, *blocks)


def add_partners(sums, rows, width):
    batch_rows = sums[0].shape[0] - rows

    def body(*refs):
        half_ref, batch_ref = refs[-2:]
        for part in range(2):
            lanes = pl.ds(part * width, width)
            both = sum(ref[:, lanes].astype(F32) for ref in refs[:-2]).astype(BF16)
            half_ref[part * rows:(part + 1) * rows, :] = both[:rows]
            batch_ref[part * batch_rows:(part + 1) * batch_rows, :] = both[rows:]

    return pl.pallas_call(
        body,
        out_shape=[jax.ShapeDtypeStruct((2 * n, width), BF16) for n in (rows, batch_rows)],
        in_specs=vmem(len(sums)),
        out_specs=vmem(2),
        compiler_params=PARAMS,
        name="add_partners",
    )(*sums)


def weights(grid, where, batch, slots, share):
    batch_rows, width = batch.shape[0] // 2, batch.shape[1]
    each = slots * 2 * share
    deep = slots * batch_rows

    def body(where_ref, batch_ref, out_ref):
        repeat = (
            lax.broadcasted_iota(jnp.int32, (batch_rows, deep), 0)
            == lax.rem(lax.broadcasted_iota(jnp.int32, (batch_rows, deep), 1), batch_rows)
        ).astype(F32).astype(BF16)
        row = lax.broadcasted_iota(jnp.int32, (each, deep), 0)
        keep = lax.rem(lax.div(row, 2 * share), slots) == lax.div(
            lax.broadcasted_iota(jnp.int32, (each, deep), 1), batch_rows
        )
        real = lax.rem(lax.div(row, share), 2) == 0
        row = lax.broadcasted_iota(jnp.int32, (each, width), 0)
        column = lax.broadcasted_iota(jnp.int32, (each, width), 1)
        for k, device in enumerate(grid.helped(where_ref[0])):
            chosen = (column == device * share + lax.rem(row, share)).astype(F32).astype(BF16)

            def spread(part):
                rows = batch_ref[part * batch_rows:(part + 1) * batch_rows, :]
                picked = lax.dot_general(chosen, rows, (((1,), (1,)), ((), ())), preferred_element_type=F32)
                return jnp.dot(picked.astype(BF16), repeat, preferred_element_type=F32)

            re, im = spread(0), spread(1)
            here = pl.ds(k * each, each)
            out_ref[here, :deep] = jnp.where(keep, jnp.where(real, re, -im), 0.0).astype(BF16)
            out_ref[here, deep:] = jnp.where(keep, jnp.where(real, im, re), 0.0).astype(BF16)

    return pl.pallas_call(
        body,
        out_shape=jax.ShapeDtypeStruct((4 * each, 2 * deep), BF16),
        in_specs=[pl.BlockSpec(memory_space=pltpu.SMEM)] + vmem(1),
        out_specs=pl.BlockSpec(memory_space=pltpu.VMEM),
        compiler_params=PARAMS,
        name="weights",
    )(where, batch)


def second_product(matrix, blocks):
    each = matrix.shape[0] // 4
    width = blocks[0].shape[1]

    def body(matrix_ref, *refs):
        block_refs, outs = refs[: len(blocks)], refs[len(blocks):]
        high = len(blocks) * each
        for number, ref in enumerate(block_refs):
            every = jnp.dot(matrix_ref[...], ref[...], preferred_element_type=F32).astype(BF16)
            for k, (out, start) in enumerate(zip((outs[0], outs[1], outs[2], outs[2]), (0, 0, 0, high))):
                start += number * each
                out[start:start + each, :] = every[k * each:(k + 1) * each]

    return pl.pallas_call(
        body,
        out_shape=[jax.ShapeDtypeStruct((n * len(blocks) * each, width), BF16) for n in (1, 1, 2)],
        in_specs=vmem(1 + len(blocks)),
        out_specs=vmem(3),
        compiler_params=PARAMS,
        name="second_product",
    )(matrix, *blocks)


def place_pairs(grid, where, groups, pair_row, pieces, share):
    width = pieces[0].shape[1]
    pairs = pair_row.shape[1]
    each = 2 * share
    slots = pairs // (4 * grid.ring)

    def body(where_ref, pair_ref, *refs):
        piece_refs, (out_ref, held, ready, leaves) = refs[: len(pieces)], refs[-4:]
        start = 0
        for number, ref in enumerate(piece_refs):
            rows = len(groups[number // 4]) * slots * each
            for tile in range(width // LANES):
                held[tile, start:start + rows, :] = ref[:rows, tile * LANES:(tile + 1) * LANES].astype(F32)
            start += rows
        row = lax.broadcasted_iota(jnp.int32, (pairs, pairs), 0)
        lane = lax.broadcasted_iota(jnp.int32, (pairs, pairs), 1)
        helpers = grid.helpers(where_ref[0])
        sources = [grid.source(helper, offset) for group in groups for helper in helpers for offset in group]
        order = lax.rem(row, slots)
        for number, source in enumerate(sources):
            order += jnp.where(lax.div(row, slots) == number, source * slots, 0)
        ordered = (order == lane).astype(F32).astype(BF16)
        paired = (pair_ref[...] == row).astype(F32).astype(BF16)
        place = lax.dot_general(ordered, paired, (((1,), (1,)), ((), ())), preferred_element_type=F32).astype(BF16)
        copies = []
        for number in range(each):
            for tile in range(width // LANES):
                rows = held[tile, pl.ds(number, pairs, stride=each), :].astype(BF16)
                placed = lax.dot_general(rows, place, (((0,), (0,)), ((), ())), preferred_element_type=F32)
                ready[number, tile * LANES:(tile + 1) * LANES, :] = placed.astype(BF16)
            copies.append(
                pltpu.make_async_copy(ready.at[number], out_ref.at[number // share, number % share], leaves.at[number])
            )
            copies[-1].start()
        for copy in copies:
            copy.wait()

    return pl.pallas_call(
        body,
        out_shape=jax.ShapeDtypeStruct((2, share, width, pairs), BF16),
        in_specs=[pl.BlockSpec(memory_space=pltpu.SMEM)] + vmem(1 + len(pieces)),
        out_specs=pl.BlockSpec(memory_space=pl.ANY),
        scratch_shapes=[
            pltpu.VMEM((width // LANES, pairs * each, LANES), F32),
            pltpu.VMEM((each, width, pairs), BF16),
            pltpu.SemaphoreType.DMA((each,)),
        ],
        compiler_params=PARAMS,
        name="place_pairs",
    )(where, pair_row, *pieces)


def on_device(n_coef, n_pair, integrals, coefficients, shell_starts, pair_ids):
    grid = Grid(n_pair)
    slots, batch_rows, ao_width = integrals.shape
    occupied = coefficients.shape[2]
    share = occupied // n_pair
    rows = slots * batch_rows
    depth = ao_width // n_pair
    piece = depth // n_coef
    assert piece % SHW == 0
    where = lax.axis_index("pair").astype(jnp.int32)[None]

    flat_ints = integrals.reshape(rows, ao_width)
    if n_coef > 1:
        coefficients = lax.all_gather(coefficients, "coef", axis=1, tiled=True)
        flat_ints = flat_ints.reshape(rows, n_coef, n_pair, piece).transpose(0, 2, 1, 3).reshape(rows, ao_width)

    def moved_to(start):
        if n_coef == 1:
            return start
        return start // piece % n_pair * depth + start // (n_pair * piece) * piece + start % piece

    reach = grid.nz
    groups = [[0, -1, 1]] + [[-step, step] for step in range(2, reach)]
    groups[-1].append(-reach)
    shared = share_integrals(grid, where, flat_ints, depth, groups)
    ints = []
    result = [None]

    def multiply(held, offsets):
        nonlocal result
        if offsets == [0]:
            return [shared[0][0]]
        if len(ints) < len(groups):
            kept, *leaving = shared[len(ints)]
            if ints:
                leaving = [after(block, held[0]) for block in leaving]
            ints.append([kept, *grid.exchange(leaving, grid.helpers)])
        last = offsets == [-reach]
        offsets = [0, *offsets] if offsets == [-1, 1] else offsets
        blocks = [held[offset] for offset in offsets]
        number = [offsets[-1] in group for group in groups].index(True)
        begin = groups[number].index(offsets[0])
        result = first_product(grid, where, offsets, ints[number], begin, shell_starts, moved_to, result[0], blocks, last)
        return ints[-1]

    gather_ring(grid, coefficients, multiply)
    kept, *leaving = result
    half_first, batch = add_partners([kept, *grid.exchange(leaving, grid.helped)], rows, occupied)
    matrix = weights(grid, where, batch, slots, share)
    pieces, groups = [], []
    before = []

    def transform(held, group):
        kept, aside, across = second_product(matrix, [held[offset] for offset in group])
        half = kept.shape[0]
        if group == [-grid.nz]:
            arrived = [kept, *grid.exchange([aside, across[:half], across[half:]], grid.helped)]
        else:
            across = grid.send(across, grid.opposite)
            arrived = [kept, grid.send(aside, grid.mate), across, grid.send(across[half:], grid.mate)]
        pieces.extend(arrived)
        groups.append(group)
        nonlocal before
        before, ready = arrived, before
        return [[kept,*ready[:3]],[kept,*ready[:3]],[kept,*ready[:3]]][len(groups) - 1] if len(groups) < 4 else []

    gather_ring(grid, half_first, transform)
    return place_pairs(grid, where, groups, pair_ids, pieces, share)


def solution(mesh):
    return jax.shard_map(
        functools.partial(on_device, mesh.shape["coef"], mesh.shape["pair"]),
        mesh=mesh,
        in_specs=(
            P(("coef", "pair"), None, None),
            P(None, ("coef", "pair"), None),
            P(),
            P("coef", None),
        ),
        out_specs=P(None, "pair", None, "coef"),
        check_vma=False,
    )
```

```python
import functools

import jax
import jax.numpy as jnp
from jax import lax
from jax.experimental import pallas as pl
from jax.experimental.pallas import tpu as pltpu
from jax.sharding import PartitionSpec as P

SHW = 4
LANES = 128
F32, BF16 = jnp.float32, jnp.bfloat16
VMEM_LIMIT = 16 * 1024 * 1024


class Grid:
    def __init__(self, n_pair):
        assert n_pair % 8 == 0
        self.nz = n_pair // 8
        self.ring = 2 * self.nz

    def device(self, spot, side, core):
        turned = (spot >= self.nz) * 1
        z = spot + turned * (self.ring - 1 - 2 * spot)
        x = turned + core * (side - turned)
        y = side + core * (turned - side)
        return ((z * 2 + y) * 2 + x) * 2 + core

    def place(self, device):
        core, x, y, z = device % 2, device // 2 % 2, device // 4 % 2, device // 8
        turned = x + core * (y - x)
        side = y + core * (x - y)
        return z + turned * (self.ring - 1 - 2 * z), side, core

    def moves(self, target):
        every = range(self.ring * 4)
        return [(device, int(self.device(*target(*self.place(device))))) for device in every]

    def sense(self, side, core):
        return (1 - 2 * core) * (1 - 2 * side)

    def around(self, way):
        return self.moves(lambda spot, side, core: ((spot + way * self.sense(side, core)) % self.ring, side, core))

    def mate(self, device):
        return device + 1 - 2 * (device % 2)

    def opposite(self, device):
        spot, side, core = self.place(device)
        return self.device(spot, 1 - side, core)

    def helpers(self, device):
        return [device, self.mate(device), self.opposite(device), self.opposite(self.mate(device))]

    def helped(self, device):
        return [device, self.mate(device), self.opposite(device), self.mate(self.opposite(device))]

    def send(self, block, target):
        return lax.ppermute(block, "pair", [(device, int(target(device))) for device in range(self.ring * 4)])

    def exchange(self, blocks, partners):
        return [self.send(block, lambda device: partners(device)[k]) for k, block in zip((1, 2, 3), blocks)]

    def spot(self, device, offset):
        spot, side, core = self.place(device)
        return (spot + offset * self.sense(side, core) + self.ring) % self.ring

    def source_at(self, device, spot):
        _, side, core = self.place(device)
        return self.device(spot, side, core)

    def source(self, device, offset):
        _, side, core = self.place(device)
        return self.device(self.spot(device, offset), side, core)


def after(value, *done):
    return lax.optimization_barrier((value, *done))[0] if done else value


def gather_ring(grid, own, meanwhile):
    around = {-1: grid.around(1), 1: grid.around(-1)}
    held, gates = {0: own}, [[]]
    for step in range(1, grid.nz + 1):
        ways = (-1, 1) if step < grid.nz else (-1,)
        for way in ways:
            block = after(held[way * (step - 1)], *gates[step - 1])
            held[way * step] = lax.ppermute(block, "pair", around[way])
        gates.append(meanwhile(held, [0] if step == 1 else [1 - step, step - 1]))
    meanwhile(held, [-grid.nz])
    return held


def vmem(count):
    return [pl.BlockSpec(memory_space=pltpu.VMEM)] * count


PARAMS = pltpu.CompilerParams(vmem_limit_bytes=VMEM_LIMIT)


def in_hbm(array):
    return pltpu.with_memory_space_constraint(array, pltpu.HBM)


def share_integrals(grid, where, batch_starts, moved_to, integrals, depth, groups):
    rows, batch_rows = integrals.shape[0], batch_starts.shape[0] * SHW

    def body(where_ref, starts_ref, ints_ref, *refs):
        outs, moved = refs[:-1], refs[-1]
        me = where_ref[0]
        copies = []
        for k, helper in enumerate(grid.helpers(me)):
            for number, group in enumerate(groups):
                for place, offset in enumerate(group):
                    start = pl.multiple_of(grid.source(helper, offset) * depth, depth)
                    out = outs[4 * number + k].at[pl.ds(0, rows), pl.ds(place * depth, depth)]
                    copies.append(
                        pltpu.make_async_copy(ints_ref.at[:, pl.ds(start, depth)], out, moved.at[len(copies)])
                    )
        for copy in copies:
            copy.start()
        row = lax.broadcasted_iota(jnp.int32, (batch_rows, depth), 0)
        wanted = row
        for shell in range(batch_starts.shape[0]):
            wanted = jnp.where(row >= shell * SHW, row + (moved_to(starts_ref[shell]) - shell * SHW), wanted)
        for number, group in enumerate(groups):
            for place, offset in enumerate(group):
                position = lax.broadcasted_iota(jnp.int32, (batch_rows, depth), 1) + grid.source(me, offset) * depth
                picks = (wanted == position).astype(F32).astype(BF16)
                outs[4 * number][rows:, place * depth:(place + 1) * depth] = picks
        for copy in copies:
            copy.wait()

    outs = pl.pallas_call(
        body,
        out_shape=[
            jax.ShapeDtypeStruct((rows + batch_rows * (k == 0), len(group) * depth), BF16)
            for group in groups
            for k in range(4)
        ],
        in_specs=[pl.BlockSpec(memory_space=pltpu.SMEM)] * 2 + [pl.BlockSpec(memory_space=pl.ANY)],
        out_specs=vmem(4 * len(groups)),
        scratch_shapes=[pltpu.SemaphoreType.DMA((4 * grid.ring,))],
        compiler_params=PARAMS,
        name="share_integrals",
    )(where, batch_starts, in_hbm(integrals))
    return [outs[4 * number:4 * number + 4] for number in range(len(groups))]


def first_product(ints, begin, total, blocks, last):
    parts, depth, width = blocks[0].shape
    rows = ints[1].shape[0]
    each = ints[0].shape[0]
    high = each + 3 * rows
    begins = total is None

    def body(*refs):
        ints_refs, refs = refs[:4], refs[4:]
        total_ref, refs = (None, refs) if begins else (refs[0], refs[1:])
        block_refs, outs = refs[: len(blocks)], refs[len(blocks):]
        sum_ref = outs[-1]
        for number, ref in enumerate(block_refs):
            columns = pl.ds((begin + number) * depth, depth)
            left = jnp.concatenate([ints_ref[:, columns] for ints_ref in ints_refs], axis=0)
            for part in range(parts):
                term = jnp.dot(left, ref[part], preferred_element_type=F32)
                lanes = pl.ds(part * width, width)
                if number > 0:
                    sum_ref[:, lanes] += term
                elif begins:
                    sum_ref[:, lanes] = term
                else:
                    sum_ref[:, lanes] = total_ref[:, lanes] + term
        if last:
            for k, out in enumerate(outs[:-1]):
                start = 0 if k == 0 else each + (k - 1) * rows
                out[:rows, :] = sum_ref[start:start + rows, :].astype(out.dtype)
                out[rows:, :] = sum_ref[rows:each, :].astype(out.dtype)

    totals = [] if begins else [total]
    whole = jax.ShapeDtypeStruct((high, parts * width), F32)
    kinds = (F32, F32, BF16, BF16)
    shapes = [jax.ShapeDtypeStruct((each, parts * width), kind) for kind in kinds] if last else [whole]
    return pl.pallas_call(
        body,
        out_shape=shapes,
        in_specs=vmem(4 + len(totals) + len(blocks)),
        out_specs=vmem(len(shapes)),
        scratch_shapes=[pltpu.VMEM(whole.shape, F32)] if last else [],
        compiler_params=PARAMS,
        cost_estimate=pl.CostEstimate(
            flops=10 * high * depth * width * parts * len(blocks), bytes_accessed=0, transcendentals=0
        ),
        name="first_product",
    )(*ints, *totals, *blocks)


def add_partners(sums, rows, width):
    batch_rows = sums[0].shape[0] - rows

    def body(*refs):
        half_ref, batch_ref = refs[-2:]
        for part in range(2):
            lanes = pl.ds(part * width, width)
            both = sum(ref[:, lanes].astype(F32) for ref in refs[:-2]).astype(BF16)
            half_ref[part * rows:(part + 1) * rows, :] = both[:rows]
            batch_ref[part * batch_rows:(part + 1) * batch_rows, :] = both[rows:]

    return pl.pallas_call(
        body,
        out_shape=[jax.ShapeDtypeStruct((2 * n, width), BF16) for n in (rows, batch_rows)],
        in_specs=vmem(len(sums)),
        out_specs=vmem(2),
        compiler_params=PARAMS,
        name="add_partners",
    )(*sums)


def weights(grid, where, batch, slots, share):
    batch_rows, width = batch.shape[0] // 2, batch.shape[1]
    each = slots * 2 * share
    deep = slots * batch_rows

    def body(where_ref, batch_ref, out_ref):
        repeat = (
            lax.broadcasted_iota(jnp.int32, (batch_rows, deep), 0)
            == lax.rem(lax.broadcasted_iota(jnp.int32, (batch_rows, deep), 1), batch_rows)
        ).astype(F32).astype(BF16)
        row = lax.broadcasted_iota(jnp.int32, (each, deep), 0)
        keep = lax.rem(lax.div(row, 2 * share), slots) == lax.div(
            lax.broadcasted_iota(jnp.int32, (each, deep), 1), batch_rows
        )
        real = lax.rem(lax.div(row, share), 2) == 0
        row = lax.broadcasted_iota(jnp.int32, (each, width), 0)
        column = lax.broadcasted_iota(jnp.int32, (each, width), 1)
        for k, device in enumerate(grid.helped(where_ref[0])):
            chosen = (column == device * share + lax.rem(row, share)).astype(F32).astype(BF16)

            def spread(part):
                rows = batch_ref[part * batch_rows:(part + 1) * batch_rows, :]
                picked = lax.dot_general(chosen, rows, (((1,), (1,)), ((), ())), preferred_element_type=F32)
                return jnp.dot(picked.astype(BF16), repeat, preferred_element_type=F32)

            re, im = spread(0), spread(1)
            here = pl.ds(k * each, each)
            out_ref[here, :deep] = jnp.where(keep, jnp.where(real, re, -im), 0.0).astype(BF16)
            out_ref[here, deep:] = jnp.where(keep, jnp.where(real, im, re), 0.0).astype(BF16)

    return pl.pallas_call(
        body,
        out_shape=jax.ShapeDtypeStruct((4 * each, 2 * deep), BF16),
        in_specs=[pl.BlockSpec(memory_space=pltpu.SMEM)] + vmem(1),
        out_specs=pl.BlockSpec(memory_space=pltpu.VMEM),
        compiler_params=PARAMS,
        name="weights",
    )(where, batch)


def second_product(matrix, blocks):
    each = matrix.shape[0] // 4
    width = blocks[0].shape[1]

    def body(matrix_ref, *refs):
        block_refs, outs = refs[: len(blocks)], refs[len(blocks):]
        high = len(blocks) * each
        for number, ref in enumerate(block_refs):
            every = jnp.dot(matrix_ref[...], ref[...], preferred_element_type=F32).astype(BF16)
            for k, (out, start) in enumerate(zip((outs[0], outs[1], outs[2], outs[2]), (0, 0, 0, high))):
                start += number * each
                out[start:start + each, :] = every[k * each:(k + 1) * each]

    return pl.pallas_call(
        body,
        out_shape=[jax.ShapeDtypeStruct((n * len(blocks) * each, width), BF16) for n in (1, 1, 2)],
        in_specs=vmem(1 + len(blocks)),
        out_specs=vmem(3),
        compiler_params=PARAMS,
        name="second_product",
    )(matrix, *blocks)


def pair_places(grid, where, groups, pair_row, slots):
    pairs = pair_row.shape[1]

    def body(where_ref, pair_ref, out_ref):
        row = lax.broadcasted_iota(jnp.int32, (pairs, pairs), 0)
        lane = lax.broadcasted_iota(jnp.int32, (pairs, pairs), 1)
        helpers = grid.helpers(where_ref[0])
        sources = [grid.source(helper, offset) for group in groups for helper in helpers for offset in group]
        order = row
        for number, source in enumerate(sources):
            order = jnp.where(row >= number * slots, row + (source - number) * slots, order)
        ordered = (order == lane).astype(F32).astype(BF16)
        paired = (pair_ref[...] == row).astype(F32).astype(BF16)
        place = lax.dot_general(ordered, paired, (((1,), (1,)), ((), ())), preferred_element_type=F32)
        out_ref[...] = place.astype(BF16)

    return pl.pallas_call(
        body,
        out_shape=jax.ShapeDtypeStruct((pairs, pairs), BF16),
        in_specs=[pl.BlockSpec(memory_space=pltpu.SMEM)] + vmem(1),
        out_specs=pl.BlockSpec(memory_space=pltpu.VMEM),
        compiler_params=PARAMS,
        name="pair_places",
    )(where, pair_row)


def place_pairs(places, groups, pieces, share):
    width = pieces[0].shape[1]
    pairs = places.shape[0]
    each = 2 * share
    slots = pairs // sum(4 * len(group) for group in groups)

    def body(place_ref, *refs):
        piece_refs, (out_ref, held, ready, leaves) = refs[: len(pieces)], refs[-4:]
        start = 0
        for number, ref in enumerate(piece_refs):
            rows = len(groups[number // 4]) * slots * each
            for tile in range(width // LANES):
                held[tile, start:start + rows, :] = ref[:rows, tile * LANES:(tile + 1) * LANES].astype(F32)
            start += rows
        place = place_ref[...]
        copies = []
        for number in range(each):
            for tile in range(width // LANES):
                rows = held[tile, pl.ds(number, pairs, stride=each), :].astype(BF16)
                placed = lax.dot_general(rows, place, (((0,), (0,)), ((), ())), preferred_element_type=F32)
                ready[number, tile * LANES:(tile + 1) * LANES, :] = placed.astype(BF16)
            copies.append(
                pltpu.make_async_copy(ready.at[number], out_ref.at[number // share, number % share], leaves.at[number])
            )
            copies[-1].start()
        for copy in copies:
            copy.wait()

    return pl.pallas_call(
        body,
        out_shape=jax.ShapeDtypeStruct((2, share, width, pairs), BF16),
        in_specs=vmem(1 + len(pieces)),
        out_specs=pl.BlockSpec(memory_space=pl.ANY),
        scratch_shapes=[
            pltpu.VMEM((width // LANES, pairs * each, LANES), F32),
            pltpu.VMEM((each, width, pairs), BF16),
            pltpu.SemaphoreType.DMA((each,)),
        ],
        compiler_params=PARAMS,
        name="place_pairs",
    )(places, *pieces)


def on_device(n_coef, n_pair, integrals, coefficients, shell_starts, pair_ids):
    grid = Grid(n_pair)
    slots, batch_rows, ao_width = integrals.shape
    occupied = coefficients.shape[2]
    share = occupied // n_pair
    rows = slots * batch_rows
    depth = ao_width // n_pair
    piece = depth // n_coef
    assert piece % SHW == 0
    where = lax.axis_index("pair").astype(jnp.int32)[None]

    flat_ints = integrals.reshape(rows, ao_width)
    if n_coef > 1:
        coefficients = lax.all_gather(coefficients, "coef", axis=1, tiled=True)
        flat_ints = flat_ints.reshape(rows, n_coef, n_pair, piece).transpose(0, 2, 1, 3).reshape(rows, ao_width)

    def moved_to(start):
        if n_coef == 1:
            return start
        return start // piece % n_pair * depth + start // (n_pair * piece) * piece + start % piece

    reach = grid.nz
    groups = [[0, -1, 1]] + [[-step, step] for step in range(2, reach)]
    groups[-1].append(-reach)
    shared = share_integrals(grid, where, shell_starts, moved_to, flat_ints, depth, groups)
    ints = []
    result = [None]

    def multiply(held, offsets):
        nonlocal result
        if offsets == [0]:
            return [shared[0][0]]
        if len(ints) < len(groups):
            kept, *leaving = shared[len(ints)]
            if ints:
                leaving = [after(block, held[0]) for block in leaving]
            ints.append([kept, *grid.exchange(leaving, grid.helpers)])
        last = offsets == [-reach]
        offsets = [0, *offsets] if offsets == [-1, 1] else offsets
        blocks = [held[offset] for offset in offsets]
        number = [offsets[-1] in group for group in groups].index(True)
        begin = groups[number].index(offsets[0])
        result = first_product(ints[number], begin, result[0], blocks, last)
        return ints[-1]

    gather_ring(grid, coefficients, multiply)
    kept, *leaving = result
    half_first, batch = add_partners([kept, *grid.exchange(leaving, grid.helped)], rows, occupied)
    matrix = weights(grid, where, batch, slots, share)
    in_order = [[0, -1, 1]] + [[-step, step] for step in range(2, grid.nz)] + [[-grid.nz]]
    places = pair_places(grid, where, in_order, pair_ids, slots)
    pieces, groups = [], []
    before = []

    def transform(held, group):
        if group == [0]:
            return [matrix, places]
        group = [0, -1, 1] if group == [-1, 1] else group
        kept, aside, across = second_product(matrix, [held[offset] for offset in group])
        half = kept.shape[0]
        if group == [-grid.nz] or group == [1 - grid.nz, grid.nz - 1]:
            arrived = [kept, *grid.exchange([aside, across[:half], across[half:]], grid.helped)]
        else:
            across = grid.send(across, grid.opposite)
            arrived = [kept, grid.send(aside, grid.mate), across, grid.send(across[half:], grid.mate)]
        pieces.extend(arrived)
        groups.append(group)
        nonlocal before
        before, ready = arrived, before
        gates = [[kept,*ready[:3]],[kept,*ready[:2]]]
        return gates[len(groups) - 1] if len(groups) <= len(gates) else []

    gather_ring(grid, half_first, transform)
    assert groups == in_order
    return place_pairs(places, groups, pieces, share)


def solution(mesh):
    return jax.shard_map(
        functools.partial(on_device, mesh.shape["coef"], mesh.shape["pair"]),
        mesh=mesh,
        in_specs=(
            P(("coef", "pair"), None, None),
            P(None, ("coef", "pair"), None),
            P(),
            P("coef", None),
        ),
        out_specs=P(None, "pair", None, "coef"),
        check_vma=False,
    )
```

```python
import functools

import jax
import jax.numpy as jnp
from jax import lax
from jax.experimental import pallas as pl
from jax.experimental.pallas import tpu as pltpu
from jax.sharding import PartitionSpec as P

SHW = 4
LANES = 128
F32, BF16 = jnp.float32, jnp.bfloat16
VMEM_LIMIT = 16 * 1024 * 1024


class Grid:
    def __init__(self, n_pair):
        assert n_pair % 8 == 0 and n_pair > 8
        self.nz = n_pair // 8
        self.ring = 2 * self.nz

    def device(self, spot, side, core):
        turned = (spot >= self.nz) * 1
        z = spot + turned * (self.ring - 1 - 2 * spot)
        x = turned + core * (side - turned)
        y = side + core * (turned - side)
        return ((z * 2 + y) * 2 + x) * 2 + core

    def place(self, device):
        core, x, y, z = device % 2, device // 2 % 2, device // 4 % 2, device // 8
        turned = x + core * (y - x)
        side = y + core * (x - y)
        return z + turned * (self.ring - 1 - 2 * z), side, core

    def moves(self, target):
        every = range(self.ring * 4)
        return [(device, int(self.device(*target(*self.place(device))))) for device in every]

    def sense(self, side, core):
        return (1 - 2 * core) * (1 - 2 * side)

    def around(self, way):
        return self.moves(lambda spot, side, core: ((spot + way * self.sense(side, core)) % self.ring, side, core))

    def mate(self, device):
        return device + 1 - 2 * (device % 2)

    def opposite(self, device):
        spot, side, core = self.place(device)
        return self.device(spot, 1 - side, core)

    def helpers(self, device):
        return [device, self.mate(device), self.opposite(device), self.opposite(self.mate(device))]

    def helped(self, device):
        return [device, self.mate(device), self.opposite(device), self.mate(self.opposite(device))]

    def send(self, block, target):
        return lax.ppermute(block, "pair", [(device, int(target(device))) for device in range(self.ring * 4)])

    def exchange(self, blocks, partners):
        return [self.send(block, lambda device: partners(device)[k]) for k, block in zip((1, 2, 3), blocks)]

    def spot(self, device, offset):
        spot, side, core = self.place(device)
        return (spot + offset * self.sense(side, core) + self.ring) % self.ring

    def source_at(self, device, spot):
        _, side, core = self.place(device)
        return self.device(spot, side, core)

    def source(self, device, offset):
        _, side, core = self.place(device)
        return self.device(self.spot(device, offset), side, core)


def after(value, *done):
    return lax.optimization_barrier((value, *done))[0] if done else value


def gather_ring(grid, own, meanwhile):
    around = {-1: grid.around(1), 1: grid.around(-1)}
    held, gates = {0: own}, [[]]
    for step in range(1, grid.nz + 1):
        ways = (-1, 1) if step < grid.nz else (-1,)
        for way in ways:
            block = after(held[way * (step - 1)], *gates[step - 1])
            held[way * step] = lax.ppermute(block, "pair", around[way])
        gates.append(meanwhile(held, [0] if step == 1 else [1 - step, step - 1]))
    meanwhile(held, [-grid.nz])
    return held


def vmem(count):
    return [pl.BlockSpec(memory_space=pltpu.VMEM)] * count


PARAMS = pltpu.CompilerParams(vmem_limit_bytes=VMEM_LIMIT)


def in_hbm(array):
    return pltpu.with_memory_space_constraint(array, pltpu.HBM)


def share_integrals(grid, where, batch_starts, moved_to, integrals, depth, groups):
    rows, batch_rows = integrals.shape[0], batch_starts.shape[0] * SHW

    def body(where_ref, starts_ref, ints_ref, *refs):
        outs, moved = refs[:-1], refs[-1]
        me = where_ref[0]
        copies = []
        for k, helper in enumerate(grid.helpers(me)):
            for number, group in enumerate(groups):
                for place, offset in enumerate(group):
                    start = pl.multiple_of(grid.source(helper, offset) * depth, depth)
                    out = outs[4 * number + k].at[pl.ds(0, rows), pl.ds(place * depth, depth)]
                    copies.append(
                        pltpu.make_async_copy(ints_ref.at[:, pl.ds(start, depth)], out, moved.at[len(copies)])
                    )
        for copy in copies:
            copy.start()
        row = lax.broadcasted_iota(jnp.int32, (batch_rows, depth), 0)
        wanted = row
        for shell in range(batch_starts.shape[0]):
            wanted = jnp.where(row >= shell * SHW, row + (moved_to(starts_ref[shell]) - shell * SHW), wanted)
        for number, group in enumerate(groups):
            for place, offset in enumerate(group):
                position = lax.broadcasted_iota(jnp.int32, (batch_rows, depth), 1) + grid.source(me, offset) * depth
                picks = (wanted == position).astype(F32).astype(BF16)
                outs[4 * number][rows:, place * depth:(place + 1) * depth] = picks
        for copy in copies:
            copy.wait()

    outs = pl.pallas_call(
        body,
        out_shape=[
            jax.ShapeDtypeStruct((rows + batch_rows * (k == 0), len(group) * depth), BF16)
            for group in groups
            for k in range(4)
        ],
        in_specs=[pl.BlockSpec(memory_space=pltpu.SMEM)] * 2 + [pl.BlockSpec(memory_space=pl.ANY)],
        out_specs=vmem(4 * len(groups)),
        scratch_shapes=[pltpu.SemaphoreType.DMA((4 * grid.ring,))],
        compiler_params=PARAMS,
        name="share_integrals",
    )(where, batch_starts, in_hbm(integrals))
    return [outs[4 * number:4 * number + 4] for number in range(len(groups))]


def first_product(ints, begin, total, blocks, last):
    parts, depth, width = blocks[0].shape
    rows = ints[1].shape[0]
    each = ints[0].shape[0]
    high = each + 3 * rows
    begins = total is None

    def body(*refs):
        ints_refs, refs = refs[:4], refs[4:]
        total_ref, refs = (None, refs) if begins else (refs[0], refs[1:])
        block_refs, outs = refs[: len(blocks)], refs[len(blocks):]
        sum_ref = outs[-1]
        for number, ref in enumerate(block_refs):
            columns = pl.ds((begin + number) * depth, depth)
            left = jnp.concatenate([ints_ref[:, columns] for ints_ref in ints_refs], axis=0)
            for part in range(parts):
                term = jnp.dot(left, ref[part], preferred_element_type=F32)
                lanes = pl.ds(part * width, width)
                if number > 0:
                    sum_ref[:, lanes] += term
                elif begins:
                    sum_ref[:, lanes] = term
                else:
                    sum_ref[:, lanes] = total_ref[:, lanes] + term
        if last:
            for k, out in enumerate(outs[:-1]):
                start = 0 if k == 0 else each + (k - 1) * rows
                out[:rows, :] = sum_ref[start:start + rows, :].astype(out.dtype)
                out[rows:, :] = sum_ref[rows:each, :].astype(out.dtype)

    totals = [] if begins else [total]
    whole = jax.ShapeDtypeStruct((high, parts * width), F32)
    kinds = (F32, F32, BF16, BF16)
    shapes = [jax.ShapeDtypeStruct((each, parts * width), kind) for kind in kinds] if last else [whole]
    return pl.pallas_call(
        body,
        out_shape=shapes,
        in_specs=vmem(4 + len(totals) + len(blocks)),
        out_specs=vmem(len(shapes)),
        scratch_shapes=[pltpu.VMEM(whole.shape, F32)] if last else [],
        compiler_params=PARAMS,
        cost_estimate=pl.CostEstimate(
            flops=10 * high * depth * width * parts * len(blocks), bytes_accessed=0, transcendentals=0
        ),
        name="first_product",
    )(*ints, *totals, *blocks)


def add_partners(sums, rows, width):
    batch_rows = sums[0].shape[0] - rows

    def body(*refs):
        half_ref, batch_ref = refs[-2:]
        for part in range(2):
            lanes = pl.ds(part * width, width)
            both = sum(ref[:, lanes].astype(F32) for ref in refs[:-2]).astype(BF16)
            half_ref[part * rows:(part + 1) * rows, :] = both[:rows]
            batch_ref[part * batch_rows:(part + 1) * batch_rows, :] = both[rows:]

    return pl.pallas_call(
        body,
        out_shape=[jax.ShapeDtypeStruct((2 * n, width), BF16) for n in (rows, batch_rows)],
        in_specs=vmem(len(sums)),
        out_specs=vmem(2),
        compiler_params=PARAMS,
        name="add_partners",
    )(*sums)


def weights(grid, where, batch, slots, share):
    batch_rows, width = batch.shape[0] // 2, batch.shape[1]
    each = slots * 2 * share
    deep = slots * batch_rows

    def body(where_ref, batch_ref, out_ref):
        repeat = (
            lax.broadcasted_iota(jnp.int32, (batch_rows, deep), 0)
            == lax.rem(lax.broadcasted_iota(jnp.int32, (batch_rows, deep), 1), batch_rows)
        ).astype(F32).astype(BF16)
        row = lax.broadcasted_iota(jnp.int32, (each, deep), 0)
        keep = lax.rem(lax.div(row, 2 * share), slots) == lax.div(
            lax.broadcasted_iota(jnp.int32, (each, deep), 1), batch_rows
        )
        real = lax.rem(lax.div(row, share), 2) == 0
        row = lax.broadcasted_iota(jnp.int32, (each, width), 0)
        column = lax.broadcasted_iota(jnp.int32, (each, width), 1)
        for k, device in enumerate(grid.helped(where_ref[0])):
            chosen = (column == device * share + lax.rem(row, share)).astype(F32).astype(BF16)

            def spread(part):
                rows = batch_ref[part * batch_rows:(part + 1) * batch_rows, :]
                picked = lax.dot_general(chosen, rows, (((1,), (1,)), ((), ())), preferred_element_type=F32)
                return jnp.dot(picked.astype(BF16), repeat, preferred_element_type=F32)

            re, im = spread(0), spread(1)
            here = pl.ds(k * each, each)
            out_ref[here, :deep] = jnp.where(keep, jnp.where(real, re, -im), 0.0).astype(BF16)
            out_ref[here, deep:] = jnp.where(keep, jnp.where(real, im, re), 0.0).astype(BF16)

    return pl.pallas_call(
        body,
        out_shape=jax.ShapeDtypeStruct((4 * each, 2 * deep), BF16),
        in_specs=[pl.BlockSpec(memory_space=pltpu.SMEM)] + vmem(1),
        out_specs=pl.BlockSpec(memory_space=pltpu.VMEM),
        compiler_params=PARAMS,
        name="weights",
    )(where, batch)


def second_product(matrix, blocks):
    each = matrix.shape[0] // 4
    width = blocks[0].shape[1]

    def body(matrix_ref, *refs):
        block_refs, outs = refs[: len(blocks)], refs[len(blocks):]
        high = len(blocks) * each
        for number, ref in enumerate(block_refs):
            every = jnp.dot(matrix_ref[...], ref[...], preferred_element_type=F32).astype(BF16)
            for k, (out, start) in enumerate(zip((outs[0], outs[1], outs[2], outs[2]), (0, 0, 0, high))):
                start += number * each
                out[start:start + each, :] = every[k * each:(k + 1) * each]

    return pl.pallas_call(
        body,
        out_shape=[jax.ShapeDtypeStruct((n * len(blocks) * each, width), BF16) for n in (1, 1, 2)],
        in_specs=vmem(1 + len(blocks)),
        out_specs=vmem(3),
        compiler_params=PARAMS,
        name="second_product",
    )(matrix, *blocks)


def pair_places(grid, where, groups, pair_row, slots):
    pairs = pair_row.shape[1]

    def body(where_ref, pair_ref, out_ref):
        row = lax.broadcasted_iota(jnp.int32, (pairs, pairs), 0)
        lane = lax.broadcasted_iota(jnp.int32, (pairs, pairs), 1)
        helpers = grid.helpers(where_ref[0])
        sources = [grid.source(helper, offset) for group in groups for helper in helpers for offset in group]
        order = row
        for number, source in enumerate(sources):
            order = jnp.where(row >= number * slots, row + (source - number) * slots, order)
        ordered = (order == lane).astype(F32).astype(BF16)
        paired = (pair_ref[...] == row).astype(F32).astype(BF16)
        place = lax.dot_general(ordered, paired, (((1,), (1,)), ((), ())), preferred_element_type=F32)
        out_ref[...] = place.astype(BF16)

    return pl.pallas_call(
        body,
        out_shape=jax.ShapeDtypeStruct((pairs, pairs), BF16),
        in_specs=[pl.BlockSpec(memory_space=pltpu.SMEM)] + vmem(1),
        out_specs=pl.BlockSpec(memory_space=pltpu.VMEM),
        compiler_params=PARAMS,
        name="pair_places",
    )(where, pair_row)


def place_pairs(places, groups, pieces, share):
    width = pieces[0].shape[1]
    pairs = places.shape[0]
    each = 2 * share
    slots = pairs // sum(4 * len(group) for group in groups)

    def body(place_ref, *refs):
        piece_refs, (out_ref, held, ready, leaves) = refs[: len(pieces)], refs[-4:]
        start = 0
        for number, ref in enumerate(piece_refs):
            rows = len(groups[number // 4]) * slots * each
            for tile in range(width // LANES):
                held[tile, start:start + rows, :] = ref[:rows, tile * LANES:(tile + 1) * LANES].astype(F32)
            start += rows
        place = place_ref[...]
        copies = []
        for number in range(each):
            for tile in range(width // LANES):
                rows = held[tile, pl.ds(number, pairs, stride=each), :].astype(BF16)
                placed = lax.dot_general(rows, place, (((0,), (0,)), ((), ())), preferred_element_type=F32)
                ready[number, tile * LANES:(tile + 1) * LANES, :] = placed.astype(BF16)
            copies.append(
                pltpu.make_async_copy(ready.at[number], out_ref.at[number // share, number % share], leaves.at[number])
            )
            copies[-1].start()
        for copy in copies:
            copy.wait()

    return pl.pallas_call(
        body,
        out_shape=jax.ShapeDtypeStruct((2, share, width, pairs), BF16),
        in_specs=vmem(1 + len(pieces)),
        out_specs=pl.BlockSpec(memory_space=pl.ANY),
        scratch_shapes=[
            pltpu.VMEM((width // LANES, (pairs + 1) * each, LANES), F32),
            pltpu.VMEM((each, width, pairs), BF16),
            pltpu.SemaphoreType.DMA((each,)),
        ],
        compiler_params=PARAMS,
        name="place_pairs",
    )(places, *pieces)


def on_device(n_coef, n_pair, integrals, coefficients, shell_starts, pair_ids):
    grid = Grid(n_pair)
    slots, batch_rows, ao_width = integrals.shape
    occupied = coefficients.shape[2]
    share = occupied // n_pair
    rows = slots * batch_rows
    depth = ao_width // n_pair
    piece = depth // n_coef
    assert piece % SHW == 0
    where = lax.axis_index("pair").astype(jnp.int32)[None]

    flat_ints = integrals.reshape(rows, ao_width)
    if n_coef > 1:
        coefficients = lax.all_gather(coefficients, "coef", axis=1, tiled=True)
        flat_ints = flat_ints.reshape(rows, n_coef, n_pair, piece).transpose(0, 2, 1, 3).reshape(rows, ao_width)

    def moved_to(start):
        if n_coef == 1:
            return start
        return start // piece % n_pair * depth + start // (n_pair * piece) * piece + start % piece

    reach = grid.nz
    groups = [[0, -1, 1]] + [[-step, step] for step in range(2, reach)]
    groups[-1].append(-reach)
    shared = share_integrals(grid, where, shell_starts, moved_to, flat_ints, depth, groups)
    ints = []
    result = [None]

    def multiply(held, offsets):
        nonlocal result
        if offsets == [0]:
            return [shared[0][0]]
        if len(ints) < len(groups):
            kept, *leaving = shared[len(ints)]
            if ints:
                leaving = [after(block, held[0]) for block in leaving]
            ints.append([kept, *grid.exchange(leaving, grid.helpers)])
        last = offsets == [-reach]
        offsets = [0, *offsets] if offsets == [-1, 1] else offsets
        blocks = [held[offset] for offset in offsets]
        number = [offsets[-1] in group for group in groups].index(True)
        begin = groups[number].index(offsets[0])
        result = first_product(ints[number], begin, result[0], blocks, last)
        return ints[-1]

    gather_ring(grid, coefficients, multiply)
    kept, *leaving = result
    half_first, batch = add_partners([kept, *grid.exchange(leaving, grid.helped)], rows, occupied)
    matrix = weights(grid, where, batch, slots, share)
    in_order = [[0, -1, 1]] + [[-step, step] for step in range(2, grid.nz)] + [[-grid.nz]]
    places = pair_places(grid, where, in_order, pair_ids, slots)
    pieces, groups = [], []
    before = []

    def transform(held, group):
        if group == [0]:
            return [matrix, places]
        group = [0, -1, 1] if group == [-1, 1] else group
        kept, aside, across = second_product(matrix, [held[offset] for offset in group])
        half = kept.shape[0]
        if group == [-grid.nz] or group == [1 - grid.nz, grid.nz - 1]:
            arrived = [kept, *grid.exchange([aside, across[:half], across[half:]], grid.helped)]
        else:
            across = grid.send(across, grid.opposite)
            arrived = [kept, grid.send(aside, grid.mate), across, grid.send(across[half:], grid.mate)]
        pieces.extend(arrived)
        groups.append(group)
        nonlocal before
        before, ready = arrived, before
        return [kept, *ready[:2]]

    gather_ring(grid, half_first, transform)
    assert groups == in_order
    return place_pairs(places, groups, pieces, share)


def solution(mesh):
    return jax.shard_map(
        functools.partial(on_device, mesh.shape["coef"], mesh.shape["pair"]),
        mesh=mesh,
        in_specs=(
            P(("coef", "pair"), None, None),
            P(None, ("coef", "pair"), None),
            P(),
            P("coef", None),
        ),
        out_specs=P(None, "pair", None, "coef"),
        check_vma=False,
    )
```

```python
import functools

import jax
import jax.numpy as jnp
from jax import lax
from jax.experimental import pallas as pl
from jax.experimental.pallas import tpu as pltpu
from jax.sharding import PartitionSpec as P

SHW = 4
LANES = 128
F32, BF16 = jnp.float32, jnp.bfloat16
VMEM_LIMIT = 16 * 1024 * 1024


class Grid:
    def __init__(self, n_pair):
        assert n_pair % 8 == 0 and n_pair > 8
        self.nz = n_pair // 8
        self.ring = 2 * self.nz

    def device(self, spot, side, core):
        turned = (spot >= self.nz) * 1
        z = spot + turned * (self.ring - 1 - 2 * spot)
        x = turned + core * (side - turned)
        y = side + core * (turned - side)
        return ((z * 2 + y) * 2 + x) * 2 + core

    def place(self, device):
        core, x, y, z = device % 2, device // 2 % 2, device // 4 % 2, device // 8
        turned = x + core * (y - x)
        side = y + core * (x - y)
        return z + turned * (self.ring - 1 - 2 * z), side, core

    def moves(self, target):
        every = range(self.ring * 4)
        return [(device, int(self.device(*target(*self.place(device))))) for device in every]

    def sense(self, side, core):
        return (1 - 2 * core) * (1 - 2 * side)

    def around(self, way):
        return self.moves(lambda spot, side, core: ((spot + way * self.sense(side, core)) % self.ring, side, core))

    def mate(self, device):
        return device + 1 - 2 * (device % 2)

    def opposite(self, device):
        spot, side, core = self.place(device)
        return self.device(spot, 1 - side, core)

    def helpers(self, device):
        return [device, self.mate(device), self.opposite(device), self.opposite(self.mate(device))]

    def helped(self, device):
        return [device, self.mate(device), self.opposite(device), self.mate(self.opposite(device))]

    def send(self, block, target):
        return lax.ppermute(block, "pair", [(device, int(target(device))) for device in range(self.ring * 4)])

    def exchange(self, blocks, partners):
        return [self.send(block, lambda device: partners(device)[k]) for k, block in zip((1, 2, 3), blocks)]

    def spot(self, device, offset):
        spot, side, core = self.place(device)
        return (spot + offset * self.sense(side, core) + self.ring) % self.ring

    def source_at(self, device, spot):
        _, side, core = self.place(device)
        return self.device(spot, side, core)

    def source(self, device, offset):
        _, side, core = self.place(device)
        return self.device(self.spot(device, offset), side, core)


def after(value, *done):
    return lax.optimization_barrier((value, *done))[0] if done else value


def gather_ring(grid, own, meanwhile):
    around = {-1: grid.around(1), 1: grid.around(-1)}
    held, gates = {0: own}, [[]]
    for step in range(1, grid.nz + 1):
        ways = (-1, 1) if step < grid.nz else (-1,)
        for way in ways:
            block = after(held[way * (step - 1)], *gates[step - 1])
            held[way * step] = lax.ppermute(block, "pair", around[way])
        gates.append(meanwhile(held, [0] if step == 1 else [1 - step, step - 1]))
    meanwhile(held, [-grid.nz])
    return held


def vmem(count):
    return [pl.BlockSpec(memory_space=pltpu.VMEM)] * count


PARAMS = pltpu.CompilerParams(vmem_limit_bytes=VMEM_LIMIT)


def in_hbm(array):
    return pltpu.with_memory_space_constraint(array, pltpu.HBM)


def share_integrals(grid, where, batch_starts, moved_to, integrals, depth, groups):
    rows, batch_rows = integrals.shape[0], batch_starts.shape[0] * SHW

    def body(where_ref, starts_ref, ints_ref, *refs):
        outs, moved = refs[:-1], refs[-1]
        me = where_ref[0]
        copies = []
        for k, helper in enumerate(grid.helpers(me)):
            for number, group in enumerate(groups):
                for place, offset in enumerate(group):
                    start = pl.multiple_of(grid.source(helper, offset) * depth, depth)
                    out = outs[4 * number + k].at[pl.ds(0, rows), pl.ds(place * depth, depth)]
                    copies.append(
                        pltpu.make_async_copy(ints_ref.at[:, pl.ds(start, depth)], out, moved.at[len(copies)])
                    )
        for copy in copies:
            copy.start()
        row = lax.broadcasted_iota(jnp.int32, (batch_rows, depth), 0)
        wanted = row
        for shell in range(batch_starts.shape[0]):
            wanted = jnp.where(row >= shell * SHW, row + (moved_to(starts_ref[shell]) - shell * SHW), wanted)
        for number, group in enumerate(groups):
            for place, offset in enumerate(group):
                position = lax.broadcasted_iota(jnp.int32, (batch_rows, depth), 1) + grid.source(me, offset) * depth
                picks = (wanted == position).astype(F32).astype(BF16)
                outs[4 * number][rows:, place * depth:(place + 1) * depth] = picks
        for copy in copies:
            copy.wait()

    outs = pl.pallas_call(
        body,
        out_shape=[
            jax.ShapeDtypeStruct((rows + batch_rows * (k == 0), len(group) * depth), BF16)
            for group in groups
            for k in range(4)
        ],
        in_specs=[pl.BlockSpec(memory_space=pltpu.SMEM)] * 2 + [pl.BlockSpec(memory_space=pl.ANY)],
        out_specs=vmem(4 * len(groups)),
        scratch_shapes=[pltpu.SemaphoreType.DMA((4 * grid.ring,))],
        compiler_params=PARAMS,
        name="share_integrals",
    )(where, batch_starts, in_hbm(integrals))
    return [outs[4 * number:4 * number + 4] for number in range(len(groups))]


def first_product(ints, begin, total, blocks, last):
    parts, depth, width = blocks[0].shape
    rows = ints[1].shape[0]
    each = ints[0].shape[0]
    high = each + 3 * rows
    begins = total is None

    def body(*refs):
        ints_refs, refs = refs[:4], refs[4:]
        total_ref, refs = (None, refs) if begins else (refs[0], refs[1:])
        block_refs, outs = refs[: len(blocks)], refs[len(blocks):]
        sum_ref = outs[-1]
        for number, ref in enumerate(block_refs):
            columns = pl.ds((begin + number) * depth, depth)
            left = jnp.concatenate([ints_ref[:, columns] for ints_ref in ints_refs], axis=0)
            for part in range(parts):
                term = jnp.dot(left, ref[part], preferred_element_type=F32)
                lanes = pl.ds(part * width, width)
                if number > 0:
                    sum_ref[:, lanes] += term
                elif begins:
                    sum_ref[:, lanes] = term
                else:
                    sum_ref[:, lanes] = total_ref[:, lanes] + term
        if last:
            for k, out in enumerate(outs[:-1]):
                start = 0 if k == 0 else each + (k - 1) * rows
                out[:rows, :] = sum_ref[start:start + rows, :].astype(out.dtype)
                out[rows:, :] = sum_ref[rows:each, :].astype(out.dtype)

    totals = [] if begins else [total]
    whole = jax.ShapeDtypeStruct((high, parts * width), F32)
    kinds = (F32, F32, BF16, BF16)
    shapes = [jax.ShapeDtypeStruct((each, parts * width), kind) for kind in kinds] if last else [whole]
    return pl.pallas_call(
        body,
        out_shape=shapes,
        in_specs=vmem(4 + len(totals) + len(blocks)),
        out_specs=vmem(len(shapes)),
        scratch_shapes=[pltpu.VMEM(whole.shape, F32)] if last else [],
        compiler_params=PARAMS,
        cost_estimate=pl.CostEstimate(
            flops=10 * high * depth * width * parts * len(blocks), bytes_accessed=0, transcendentals=0
        ),
        name="first_product",
    )(*ints, *totals, *blocks)


def add_partners(sums, rows, width):
    batch_rows = sums[0].shape[0] - rows

    def body(*refs):
        half_ref, batch_ref = refs[-2:]
        for part in range(2):
            lanes = pl.ds(part * width, width)
            both = sum(ref[:, lanes].astype(F32) for ref in refs[:-2]).astype(BF16)
            half_ref[part * rows:(part + 1) * rows, :] = both[:rows]
            batch_ref[part * batch_rows:(part + 1) * batch_rows, :] = both[rows:]

    return pl.pallas_call(
        body,
        out_shape=[jax.ShapeDtypeStruct((2 * n, width), BF16) for n in (rows, batch_rows)],
        in_specs=vmem(len(sums)),
        out_specs=vmem(2),
        compiler_params=PARAMS,
        name="add_partners",
    )(*sums)


def weights(grid, where, batch, slots, share):
    batch_rows, width = batch.shape[0] // 2, batch.shape[1]
    each = slots * 2 * share
    deep = slots * batch_rows

    def body(where_ref, batch_ref, out_ref):
        repeat = (
            lax.broadcasted_iota(jnp.int32, (batch_rows, deep), 0)
            == lax.rem(lax.broadcasted_iota(jnp.int32, (batch_rows, deep), 1), batch_rows)
        ).astype(F32).astype(BF16)
        row = lax.broadcasted_iota(jnp.int32, (each, deep), 0)
        keep = lax.rem(lax.div(row, 2 * share), slots) == lax.div(
            lax.broadcasted_iota(jnp.int32, (each, deep), 1), batch_rows
        )
        real = lax.rem(lax.div(row, share), 2) == 0
        row = lax.broadcasted_iota(jnp.int32, (each, width), 0)
        column = lax.broadcasted_iota(jnp.int32, (each, width), 1)
        for k, device in enumerate(grid.helped(where_ref[0])):
            chosen = (column == device * share + lax.rem(row, share)).astype(F32).astype(BF16)

            def spread(part):
                rows = batch_ref[part * batch_rows:(part + 1) * batch_rows, :]
                picked = lax.dot_general(chosen, rows, (((1,), (1,)), ((), ())), preferred_element_type=F32)
                return jnp.dot(picked.astype(BF16), repeat, preferred_element_type=F32)

            re, im = spread(0), spread(1)
            here = pl.ds(k * each, each)
            out_ref[here, :deep] = jnp.where(keep, jnp.where(real, re, -im), 0.0).astype(BF16)
            out_ref[here, deep:] = jnp.where(keep, jnp.where(real, im, re), 0.0).astype(BF16)

    return pl.pallas_call(
        body,
        out_shape=jax.ShapeDtypeStruct((4 * each, 2 * deep), BF16),
        in_specs=[pl.BlockSpec(memory_space=pltpu.SMEM)] + vmem(1),
        out_specs=pl.BlockSpec(memory_space=pltpu.VMEM),
        compiler_params=PARAMS,
        name="weights",
    )(where, batch)


def second_product(matrix, blocks):
    each = matrix.shape[0] // 4
    width = blocks[0].shape[1]

    def body(matrix_ref, *refs):
        block_refs, outs = refs[: len(blocks)], refs[len(blocks):]
        high = len(blocks) * each
        for number, ref in enumerate(block_refs):
            every = jnp.dot(matrix_ref[...], ref[...], preferred_element_type=F32).astype(BF16)
            for k, (out, start) in enumerate(zip((outs[0], outs[1], outs[2], outs[2]), (0, 0, 0, high))):
                start += number * each
                out[start:start + each, :] = every[k * each:(k + 1) * each]

    return pl.pallas_call(
        body,
        out_shape=[jax.ShapeDtypeStruct((n * len(blocks) * each, width), BF16) for n in (1, 1, 2)],
        in_specs=vmem(1 + len(blocks)),
        out_specs=vmem(3),
        compiler_params=PARAMS,
        name="second_product",
    )(matrix, *blocks)


def pair_places(grid, where, groups, pair_row, slots):
    pairs = pair_row.shape[1]

    def body(where_ref, pair_ref, out_ref):
        row = lax.broadcasted_iota(jnp.int32, (pairs, pairs), 0)
        lane = lax.broadcasted_iota(jnp.int32, (pairs, pairs), 1)
        helpers = grid.helpers(where_ref[0])
        sources = [grid.source(helper, offset) for group in groups for helper in helpers for offset in group]
        order = row
        for number, source in enumerate(sources):
            order = jnp.where(row >= number * slots, row + (source - number) * slots, order)
        ordered = (order == lane).astype(F32).astype(BF16)
        paired = (pair_ref[...] == row).astype(F32).astype(BF16)
        place = lax.dot_general(ordered, paired, (((1,), (1,)), ((), ())), preferred_element_type=F32)
        out_ref[...] = place.astype(BF16)

    return pl.pallas_call(
        body,
        out_shape=jax.ShapeDtypeStruct((pairs, pairs), BF16),
        in_specs=[pl.BlockSpec(memory_space=pltpu.SMEM)] + vmem(1),
        out_specs=pl.BlockSpec(memory_space=pltpu.VMEM),
        compiler_params=PARAMS,
        name="pair_places",
    )(where, pair_row)


def widen(pieces, high):
    tiles = pieces[0].shape[1] // LANES

    def body(*refs):
        for number, ref in enumerate(refs[:-1]):
            for tile in range(tiles):
                lanes = pl.ds(tile * LANES, LANES)
                refs[-1][tile, number * high:(number + 1) * high, :] = ref[:high, lanes].astype(F32)

    return pl.pallas_call(
        body,
        out_shape=jax.ShapeDtypeStruct((tiles, len(pieces) * high + high, LANES), F32),
        in_specs=vmem(len(pieces)),
        out_specs=pl.BlockSpec(memory_space=pltpu.VMEM),
        compiler_params=PARAMS,
        name="widen",
    )(*pieces)


def place_pairs(places, groups, pieces, share):
    width = pieces[0].shape[1]
    pairs = places.shape[0]
    each = 2 * share
    early = pieces[0].shape[0] * 4
    wide, pieces = widen(pieces[:4], pieces[0].shape[0]), pieces[4:]
    before = early // each
    slots = pairs // sum(4 * len(group) for group in groups)

    def body(place_ref, wide_ref, *refs):
        piece_refs, (out_ref, held, ready, leaves) = refs[: len(pieces)], refs[-4:]
        start = 0
        for number, ref in enumerate(piece_refs):
            rows = len(groups[1 + number // 4]) * slots * each
            for tile in range(width // LANES):
                held[tile, start:start + rows, :] = ref[:rows, tile * LANES:(tile + 1) * LANES].astype(F32)
            start += rows
        place = place_ref[...]
        copies = []
        for number in range(each):
            for tile in range(width // LANES):
                first = wide_ref[tile, pl.ds(number, before, stride=each), :]
                later = held[tile, pl.ds(number, pairs - before, stride=each), :]
                rows = jnp.concatenate([first, later], axis=0).astype(BF16)
                placed = lax.dot_general(rows, place, (((0,), (0,)), ((), ())), preferred_element_type=F32)
                ready[number, tile * LANES:(tile + 1) * LANES, :] = placed.astype(BF16)
            copies.append(
                pltpu.make_async_copy(ready.at[number], out_ref.at[number // share, number % share], leaves.at[number])
            )
            copies[-1].start()
        for copy in copies:
            copy.wait()

    return pl.pallas_call(
        body,
        out_shape=jax.ShapeDtypeStruct((2, share, width, pairs), BF16),
        in_specs=vmem(2 + len(pieces)),
        out_specs=pl.BlockSpec(memory_space=pl.ANY),
        scratch_shapes=[
            pltpu.VMEM((width // LANES, (pairs - before + 1) * each, LANES), F32),
            pltpu.VMEM((each, width, pairs), BF16),
            pltpu.SemaphoreType.DMA((each,)),
        ],
        compiler_params=PARAMS,
        name="place_pairs",
    )(places, wide, *pieces)


def on_device(n_coef, n_pair, integrals, coefficients, shell_starts, pair_ids):
    grid = Grid(n_pair)
    slots, batch_rows, ao_width = integrals.shape
    occupied = coefficients.shape[2]
    share = occupied // n_pair
    rows = slots * batch_rows
    depth = ao_width // n_pair
    piece = depth // n_coef
    assert piece % SHW == 0
    where = lax.axis_index("pair").astype(jnp.int32)[None]

    flat_ints = integrals.reshape(rows, ao_width)
    if n_coef > 1:
        coefficients = lax.all_gather(coefficients, "coef", axis=1, tiled=True)
        flat_ints = flat_ints.reshape(rows, n_coef, n_pair, piece).transpose(0, 2, 1, 3).reshape(rows, ao_width)

    def moved_to(start):
        if n_coef == 1:
            return start
        return start // piece % n_pair * depth + start // (n_pair * piece) * piece + start % piece

    reach = grid.nz
    groups = [[0, -1, 1]] + [[-step, step] for step in range(2, reach)]
    groups[-1].append(-reach)
    shared = share_integrals(grid, where, shell_starts, moved_to, flat_ints, depth, groups)
    ints = []
    result = [None]

    def multiply(held, offsets):
        nonlocal result
        if offsets == [0]:
            return [shared[0][0]]
        if len(ints) < len(groups):
            kept, *leaving = shared[len(ints)]
            ints.append([kept, *grid.exchange(leaving, grid.helpers)])
        last = offsets == [-reach]
        offsets = [0, *offsets] if offsets == [-1, 1] else offsets
        blocks = [held[offset] for offset in offsets]
        number = [offsets[-1] in group for group in groups].index(True)
        begin = groups[number].index(offsets[0])
        result = first_product(ints[number], begin, result[0], blocks, last)
        return ints[-1]

    gather_ring(grid, coefficients, multiply)
    kept, *leaving = result
    half_first, batch = add_partners([kept, *grid.exchange(leaving, grid.helped)], rows, occupied)
    matrix = weights(grid, where, batch, slots, share)
    in_order = [[0, -1, 1]] + [[-step, step] for step in range(2, grid.nz)] + [[-grid.nz]]
    places = pair_places(grid, where, in_order, pair_ids, slots)
    pieces, groups = [], []
    before = []

    def transform(held, group):
        if group == [0]:
            return [matrix, places]
        group = [0, -1, 1] if group == [-1, 1] else group
        kept, aside, across = second_product(matrix, [held[offset] for offset in group])
        half = kept.shape[0]
        if group == [-grid.nz] or group == [1 - grid.nz, grid.nz - 1]:
            arrived = [kept, *grid.exchange([aside, across[:half], across[half:]], grid.helped)]
        else:
            across = grid.send(across, grid.opposite)
            arrived = [kept, grid.send(aside, grid.mate), across, grid.send(across[half:], grid.mate)]
        pieces.extend(arrived)
        groups.append(group)
        nonlocal before
        before, ready = arrived, before
        return [kept, *ready[:2]]

    gather_ring(grid, half_first, transform)
    assert groups == in_order
    return place_pairs(places, groups, pieces, share)


def solution(mesh):
    return jax.shard_map(
        functools.partial(on_device, mesh.shape["coef"], mesh.shape["pair"]),
        mesh=mesh,
        in_specs=(
            P(("coef", "pair"), None, None),
            P(None, ("coef", "pair"), None),
            P(),
            P("coef", None),
        ),
        out_specs=P(None, "pair", None, "coef"),
        check_vma=False,
    )
```

```python
import functools

import jax
import jax.numpy as jnp
from jax import lax
from jax.experimental import pallas as pl
from jax.experimental.pallas import tpu as pltpu
from jax.sharding import PartitionSpec as P

SHW = 4
LANES = 128
F32, BF16 = jnp.float32, jnp.bfloat16
VMEM_LIMIT = 16 * 1024 * 1024


class Grid:
    def __init__(self, n_pair):
        assert n_pair % 8 == 0 and n_pair > 8
        self.nz = n_pair // 8
        self.ring = 2 * self.nz

    def device(self, spot, side, core):
        turned = (spot >= self.nz) * 1
        z = spot + turned * (self.ring - 1 - 2 * spot)
        x = turned + core * (side - turned)
        y = side + core * (turned - side)
        return ((z * 2 + y) * 2 + x) * 2 + core

    def place(self, device):
        core, x, y, z = device % 2, device // 2 % 2, device // 4 % 2, device // 8
        turned = x + core * (y - x)
        side = y + core * (x - y)
        return z + turned * (self.ring - 1 - 2 * z), side, core

    def moves(self, target):
        every = range(self.ring * 4)
        return [(device, int(self.device(*target(*self.place(device))))) for device in every]

    def sense(self, side, core):
        return (1 - 2 * core) * (1 - 2 * side)

    def around(self, way):
        return self.moves(lambda spot, side, core: ((spot + way * self.sense(side, core)) % self.ring, side, core))

    def mate(self, device):
        return device + 1 - 2 * (device % 2)

    def opposite(self, device):
        spot, side, core = self.place(device)
        return self.device(spot, 1 - side, core)

    def helpers(self, device):
        return [device, self.mate(device), self.opposite(device), self.opposite(self.mate(device))]

    def helped(self, device):
        return [device, self.mate(device), self.opposite(device), self.mate(self.opposite(device))]

    def send(self, block, target):
        return lax.ppermute(block, "pair", [(device, int(target(device))) for device in range(self.ring * 4)])

    def exchange(self, blocks, partners):
        return [self.send(block, lambda device: partners(device)[k]) for k, block in zip((1, 2, 3), blocks)]

    def spot(self, device, offset):
        spot, side, core = self.place(device)
        return (spot + offset * self.sense(side, core) + self.ring) % self.ring

    def source_at(self, device, spot):
        _, side, core = self.place(device)
        return self.device(spot, side, core)

    def source(self, device, offset):
        _, side, core = self.place(device)
        return self.device(self.spot(device, offset), side, core)


def after(value, *done):
    return lax.optimization_barrier((value, *done))[0] if done else value


def gather_ring(grid, own, meanwhile):
    around = {-1: grid.around(1), 1: grid.around(-1)}
    held, gates = {0: own}, [[]]
    for step in range(1, grid.nz + 1):
        ways = (1, -1) if step < grid.nz else (-1,)
        for way in ways:
            block = after(held[way * (step - 1)], *gates[step - 1])
            held[way * step] = lax.ppermute(block, "pair", around[way])
        gates.append(meanwhile(held, [0] if step == 1 else [1 - step, step - 1]))
    meanwhile(held, [-grid.nz])
    return held


def vmem(count):
    return [pl.BlockSpec(memory_space=pltpu.VMEM)] * count


PARAMS = pltpu.CompilerParams(vmem_limit_bytes=VMEM_LIMIT)


def in_hbm(array):
    return pltpu.with_memory_space_constraint(array, pltpu.HBM)


def share_integrals(grid, where, batch_starts, moved_to, integrals, depth, groups):
    rows, batch_rows = integrals.shape[0], batch_starts.shape[0] * SHW

    def body(where_ref, starts_ref, ints_ref, *refs):
        outs, moved = refs[:-1], refs[-1]
        me = where_ref[0]
        copies = []
        for k, helper in enumerate(grid.helpers(me)):
            for number, group in enumerate(groups):
                for place, offset in enumerate(group):
                    start = pl.multiple_of(grid.source(helper, offset) * depth, depth)
                    out = outs[4 * number + k].at[pl.ds(0, rows), pl.ds(place * depth, depth)]
                    copies.append(
                        pltpu.make_async_copy(ints_ref.at[:, pl.ds(start, depth)], out, moved.at[len(copies)])
                    )
        for copy in copies:
            copy.start()
        row = lax.broadcasted_iota(jnp.int32, (batch_rows, depth), 0)
        wanted = row
        for shell in range(batch_starts.shape[0]):
            wanted = jnp.where(row >= shell * SHW, row + (moved_to(starts_ref[shell]) - shell * SHW), wanted)
        for number, group in enumerate(groups):
            for place, offset in enumerate(group):
                position = lax.broadcasted_iota(jnp.int32, (batch_rows, depth), 1) + grid.source(me, offset) * depth
                picks = (wanted == position).astype(F32).astype(BF16)
                outs[4 * number][rows:, place * depth:(place + 1) * depth] = picks
        for copy in copies:
            copy.wait()

    outs = pl.pallas_call(
        body,
        out_shape=[
            jax.ShapeDtypeStruct((rows + batch_rows * (k == 0), len(group) * depth), BF16)
            for group in groups
            for k in range(4)
        ],
        in_specs=[pl.BlockSpec(memory_space=pltpu.SMEM)] * 2 + [pl.BlockSpec(memory_space=pl.ANY)],
        out_specs=vmem(4 * len(groups)),
        scratch_shapes=[pltpu.SemaphoreType.DMA((4 * grid.ring,))],
        compiler_params=PARAMS,
        name="share_integrals",
    )(where, batch_starts, in_hbm(integrals))
    return [outs[4 * number:4 * number + 4] for number in range(len(groups))]


def first_product(ints, begin, total, blocks, last):
    parts, depth, width = blocks[0].shape
    rows = ints[1].shape[0]
    each = ints[0].shape[0]
    high = each + 3 * rows
    begins = total is None

    def body(*refs):
        ints_refs, refs = refs[:4], refs[4:]
        total_ref, refs = (None, refs) if begins else (refs[0], refs[1:])
        block_refs, outs = refs[: len(blocks)], refs[len(blocks):]
        sum_ref = outs[-1]
        for number, ref in enumerate(block_refs):
            columns = pl.ds((begin + number) * depth, depth)
            left = jnp.concatenate([ints_ref[:, columns] for ints_ref in ints_refs], axis=0)
            for part in range(parts):
                term = jnp.dot(left, ref[part], preferred_element_type=F32)
                lanes = pl.ds(part * width, width)
                if number > 0:
                    sum_ref[:, lanes] += term
                elif begins:
                    sum_ref[:, lanes] = term
                else:
                    sum_ref[:, lanes] = total_ref[:, lanes] + term
        if last:
            for k, out in enumerate(outs[:-1]):
                start = 0 if k == 0 else each + (k - 1) * rows
                out[:rows, :] = sum_ref[start:start + rows, :].astype(out.dtype)
                out[rows:, :] = sum_ref[rows:each, :].astype(out.dtype)

    totals = [] if begins else [total]
    whole = jax.ShapeDtypeStruct((high, parts * width), F32)
    kinds = (F32, F32, BF16, BF16)
    shapes = [jax.ShapeDtypeStruct((each, parts * width), kind) for kind in kinds] if last else [whole]
    return pl.pallas_call(
        body,
        out_shape=shapes,
        in_specs=vmem(4 + len(totals) + len(blocks)),
        out_specs=vmem(len(shapes)),
        scratch_shapes=[pltpu.VMEM(whole.shape, F32)] if last else [],
        compiler_params=PARAMS,
        cost_estimate=pl.CostEstimate(
            flops=10 * high * depth * width * parts * len(blocks), bytes_accessed=0, transcendentals=0
        ),
        name="first_product",
    )(*ints, *totals, *blocks)


def add_partners(sums, rows, width):
    batch_rows = sums[0].shape[0] - rows

    def body(*refs):
        half_ref, batch_ref = refs[-2:]
        for part in range(2):
            lanes = pl.ds(part * width, width)
            both = sum(ref[:, lanes].astype(F32) for ref in refs[:-2]).astype(BF16)
            half_ref[part * rows:(part + 1) * rows, :] = both[:rows]
            batch_ref[part * batch_rows:(part + 1) * batch_rows, :] = both[rows:]

    return pl.pallas_call(
        body,
        out_shape=[jax.ShapeDtypeStruct((2 * n, width), BF16) for n in (rows, batch_rows)],
        in_specs=vmem(len(sums)),
        out_specs=vmem(2),
        compiler_params=PARAMS,
        name="add_partners",
    )(*sums)


def weights(grid, where, batch, slots, share):
    batch_rows, width = batch.shape[0] // 2, batch.shape[1]
    each = slots * 2 * share
    deep = slots * batch_rows

    def body(where_ref, batch_ref, out_ref):
        repeat = (
            lax.broadcasted_iota(jnp.int32, (batch_rows, deep), 0)
            == lax.rem(lax.broadcasted_iota(jnp.int32, (batch_rows, deep), 1), batch_rows)
        ).astype(F32).astype(BF16)
        row = lax.broadcasted_iota(jnp.int32, (each, deep), 0)
        keep = lax.rem(lax.div(row, 2 * share), slots) == lax.div(
            lax.broadcasted_iota(jnp.int32, (each, deep), 1), batch_rows
        )
        real = lax.rem(lax.div(row, share), 2) == 0
        row = lax.broadcasted_iota(jnp.int32, (each, width), 0)
        column = lax.broadcasted_iota(jnp.int32, (each, width), 1)
        for k, device in enumerate(grid.helped(where_ref[0])):
            chosen = (column == device * share + lax.rem(row, share)).astype(F32).astype(BF16)

            def spread(part):
                rows = batch_ref[part * batch_rows:(part + 1) * batch_rows, :]
                picked = lax.dot_general(chosen, rows, (((1,), (1,)), ((), ())), preferred_element_type=F32)
                return jnp.dot(picked.astype(BF16), repeat, preferred_element_type=F32)

            re, im = spread(0), spread(1)
            here = pl.ds(k * each, each)
            out_ref[here, :deep] = jnp.where(keep, jnp.where(real, re, -im), 0.0).astype(BF16)
            out_ref[here, deep:] = jnp.where(keep, jnp.where(real, im, re), 0.0).astype(BF16)

    return pl.pallas_call(
        body,
        out_shape=jax.ShapeDtypeStruct((4 * each, 2 * deep), BF16),
        in_specs=[pl.BlockSpec(memory_space=pltpu.SMEM)] + vmem(1),
        out_specs=pl.BlockSpec(memory_space=pltpu.VMEM),
        compiler_params=PARAMS,
        name="weights",
    )(where, batch)


def second_product(matrix, blocks):
    each = matrix.shape[0] // 4
    width = blocks[0].shape[1]

    def body(matrix_ref, *refs):
        block_refs, outs = refs[: len(blocks)], refs[len(blocks):]
        high = len(blocks) * each
        for number, ref in enumerate(block_refs):
            every = jnp.dot(matrix_ref[...], ref[...], preferred_element_type=F32).astype(BF16)
            for k, (out, start) in enumerate(zip((outs[0], outs[1], outs[2], outs[2]), (0, 0, 0, high))):
                start += number * each
                out[start:start + each, :] = every[k * each:(k + 1) * each]

    return pl.pallas_call(
        body,
        out_shape=[jax.ShapeDtypeStruct((n * len(blocks) * each, width), BF16) for n in (1, 1, 2)],
        in_specs=vmem(1 + len(blocks)),
        out_specs=vmem(3),
        compiler_params=PARAMS,
        name="second_product",
    )(matrix, *blocks)


def pair_places(grid, where, groups, pair_row, slots):
    pairs = pair_row.shape[1]

    def body(where_ref, pair_ref, out_ref):
        row = lax.broadcasted_iota(jnp.int32, (pairs, pairs), 0)
        lane = lax.broadcasted_iota(jnp.int32, (pairs, pairs), 1)
        helpers = grid.helpers(where_ref[0])
        sources = [grid.source(helper, offset) for group in groups for helper in helpers for offset in group]
        order = row
        for number, source in enumerate(sources):
            order = jnp.where(row >= number * slots, row + (source - number) * slots, order)
        ordered = (order == lane).astype(F32).astype(BF16)
        paired = (pair_ref[...] == row).astype(F32).astype(BF16)
        place = lax.dot_general(ordered, paired, (((1,), (1,)), ((), ())), preferred_element_type=F32)
        out_ref[...] = place.astype(BF16)

    return pl.pallas_call(
        body,
        out_shape=jax.ShapeDtypeStruct((pairs, pairs), BF16),
        in_specs=[pl.BlockSpec(memory_space=pltpu.SMEM)] + vmem(1),
        out_specs=pl.BlockSpec(memory_space=pltpu.VMEM),
        compiler_params=PARAMS,
        name="pair_places",
    )(where, pair_row)


def widen(pieces, high):
    tiles = pieces[0].shape[1] // LANES

    def body(*refs):
        for number, ref in enumerate(refs[:-1]):
            for tile in range(tiles):
                lanes = pl.ds(tile * LANES, LANES)
                refs[-1][tile, number * high:(number + 1) * high, :] = ref[:high, lanes].astype(F32)

    return pl.pallas_call(
        body,
        out_shape=jax.ShapeDtypeStruct((tiles, len(pieces) * high + high, LANES), F32),
        in_specs=vmem(len(pieces)),
        out_specs=pl.BlockSpec(memory_space=pltpu.VMEM),
        compiler_params=PARAMS,
        name="widen",
    )(*pieces)


def place_pairs(places, groups, pieces, share):
    width = pieces[0].shape[1]
    pairs = places.shape[0]
    each = 2 * share
    early = pieces[0].shape[0] * 4
    wide, pieces = widen(pieces[:4], pieces[0].shape[0]), pieces[4:]
    before = early // each
    slots = pairs // sum(4 * len(group) for group in groups)

    def body(place_ref, wide_ref, *refs):
        piece_refs, (out_ref, held, ready, leaves) = refs[: len(pieces)], refs[-4:]
        start = 0
        for number, ref in enumerate(piece_refs):
            rows = len(groups[1 + number // 4]) * slots * each
            for tile in range(width // LANES):
                held[tile, start:start + rows, :] = ref[:rows, tile * LANES:(tile + 1) * LANES].astype(F32)
            start += rows
        place = place_ref[...]
        copies = []
        for number in range(each):
            for tile in range(width // LANES):
                first = wide_ref[tile, pl.ds(number, before, stride=each), :]
                later = held[tile, pl.ds(number, pairs - before, stride=each), :]
                rows = jnp.concatenate([first, later], axis=0).astype(BF16)
                placed = lax.dot_general(rows, place, (((0,), (0,)), ((), ())), preferred_element_type=F32)
                ready[number, tile * LANES:(tile + 1) * LANES, :] = placed.astype(BF16)
            copies.append(
                pltpu.make_async_copy(ready.at[number], out_ref.at[number // share, number % share], leaves.at[number])
            )
            copies[-1].start()
        for copy in copies:
            copy.wait()

    return pl.pallas_call(
        body,
        out_shape=jax.ShapeDtypeStruct((2, share, width, pairs), BF16),
        in_specs=vmem(2 + len(pieces)),
        out_specs=pl.BlockSpec(memory_space=pl.ANY),
        scratch_shapes=[
            pltpu.VMEM((width // LANES, (pairs - before + 1) * each, LANES), F32),
            pltpu.VMEM((each, width, pairs), BF16),
            pltpu.SemaphoreType.DMA((each,)),
        ],
        compiler_params=PARAMS,
        name="place_pairs",
    )(places, wide, *pieces)


def on_device(n_coef, n_pair, integrals, coefficients, shell_starts, pair_ids):
    grid = Grid(n_pair)
    slots, batch_rows, ao_width = integrals.shape
    occupied = coefficients.shape[2]
    share = occupied // n_pair
    rows = slots * batch_rows
    depth = ao_width // n_pair
    piece = depth // n_coef
    assert piece % SHW == 0
    where = lax.axis_index("pair").astype(jnp.int32)[None]

    flat_ints = integrals.reshape(rows, ao_width)
    if n_coef > 1:
        coefficients = lax.all_gather(coefficients, "coef", axis=1, tiled=True)
        flat_ints = flat_ints.reshape(rows, n_coef, n_pair, piece).transpose(0, 2, 1, 3).reshape(rows, ao_width)

    def moved_to(start):
        if n_coef == 1:
            return start
        return start // piece % n_pair * depth + start // (n_pair * piece) * piece + start % piece

    reach = grid.nz
    groups = [[0, -1, 1]] + [[-step, step] for step in range(2, reach)]
    groups[-1].append(-reach)
    shared = share_integrals(grid, where, shell_starts, moved_to, flat_ints, depth, groups)
    ints = []
    result = [None]

    def multiply(held, offsets):
        nonlocal result
        if offsets == [0]:
            return [shared[0][0]]
        if len(ints) < len(groups):
            kept, *leaving = shared[len(ints)]
            ints.append([kept, *grid.exchange(leaving, grid.helpers)])
        last = offsets == [-reach]
        offsets = [0, *offsets] if offsets == [-1, 1] else offsets
        blocks = [held[offset] for offset in offsets]
        number = [offsets[-1] in group for group in groups].index(True)
        begin = groups[number].index(offsets[0])
        result = first_product(ints[number], begin, result[0], blocks, last)
        return ints[-1]

    gather_ring(grid, coefficients, multiply)
    kept, *leaving = result
    half_first, batch = add_partners([kept, *grid.exchange(leaving, grid.helped)], rows, occupied)
    matrix = weights(grid, where, batch, slots, share)
    in_order = [[0, -1, 1]] + [[-step, step] for step in range(2, grid.nz)] + [[-grid.nz]]
    places = pair_places(grid, where, in_order, pair_ids, slots)
    pieces, groups = [], []
    before = []

    def transform(held, group):
        if group == [0]:
            return [matrix, places]
        group = [0, -1, 1] if group == [-1, 1] else group
        kept, aside, across = second_product(matrix, [held[offset] for offset in group])
        half = kept.shape[0]
        if group == [-grid.nz] or group == [1 - grid.nz, grid.nz - 1]:
            arrived = [kept, *grid.exchange([aside, across[:half], across[half:]], grid.helped)]
        else:
            across = grid.send(across, grid.opposite)
            arrived = [kept, grid.send(aside, grid.mate), across, grid.send(across[half:], grid.mate)]
        pieces.extend(arrived)
        groups.append(group)
        nonlocal before
        before, ready = arrived, before
        return [kept, *ready[:2]]

    gather_ring(grid, half_first, transform)
    assert groups == in_order
    return place_pairs(places, groups, pieces, share)


def solution(mesh):
    return jax.shard_map(
        functools.partial(on_device, mesh.shape["coef"], mesh.shape["pair"]),
        mesh=mesh,
        in_specs=(
            P(("coef", "pair"), None, None),
            P(None, ("coef", "pair"), None),
            P(),
            P("coef", None),
        ),
        out_specs=P(None, "pair", None, "coef"),
        check_vma=False,
    )
```
